32 devices in a mesh: ctx: 8 (over y, x, core), exp: 4 (over z).
Axes of the slice: x: 2, y: 2, z: 4, core: 2. Of those that a mesh axis runs over, the one named last changes fastest.
Arguments:
- mixer_x: bfloat16 [1024, 4096], P('ctx', 'exp')
- mixer_z: bfloat16 [1024, 4096], P('ctx', 'exp'), may hold values from -6 to 6
- step_raw: float32 [1024, 4096], P('ctx', 'exp')
- input_b: float32 [16, 1024], P(None, 'ctx'), may hold values from -6 to 6
- output_c: float32 [16, 1024], P(None, 'ctx'), may hold values from -4 to 4
- decay_log: float32 [16, 4096], P(None, 'exp')
- skip_gain: float32 [4096], P('exp'), may hold values from 0.5 to 1.5
- out_proj: bfloat16 [4096, 2048], P('exp'), may hold values from -0.09375 to 0.09375
- residual: bfloat16 [1024, 2048], P(('ctx', 'exp')), may hold values from -6 to 6
- norm_gain: float32 [2048], replicated, may hold values from 0.1 to 1.9
- gate_proj: bfloat16 [4, 2048, 8192], P('exp', None, 'ctx'), may hold values from -0.125 to 0.125
- up_proj: bfloat16 [4, 2048, 8192], P('exp', None, 'ctx'), may hold values from -0.125 to 0.125
- down_proj: bfloat16 [4, 8192, 2048], P('exp', 'ctx'), may hold values from -0.0625 to 0.0625
- expert_ids: int32 [1024, 2], P(('ctx', 'exp')), may hold values from 0 to 3, as said below
- slot_ids: int32 [1024, 2], P(('ctx', 'exp')), may hold values from -1 to 15, as said below
- route_weight: float32 [1024, 2], P(('ctx', 'exp')), may hold values from 0.2 to 1
Outputs:
- layer_out: bfloat16 [1024, 2048], P(('ctx', 'exp'))
The draws below stay inside these ranges and needn't reach their ends.
Inputs may be any that keep to these rules, and one draw needn't show every extreme that they name: `expert_ids`: A token's two ids differ. In every draw one expert is named by at least 16 tokens of every device's 32 tokens. `slot_ids`: A copy's slot is its rank among the copies of the same device's tokens to the same expert, taken in order of token and then of choice, or -1 where that rank is 16 or more.
All inputs are finite; a program needn't handle non-finite values.
Results may differ from the reference program's by a relative error of at most 0.017.
Values may be sent and summed in bfloat16 or wider, within the bound.
A program may use at most 64 MiB of HBM per device.

```python
import math
import jax
import jax.numpy as jnp
from jax import lax

D = 2048
INNER = 4096
STATE = 16
FF = 8192
TOP = 2
EXPERTS = 4
SEQ = 1024
TOK_DEV = 32
CAP = 16
N_CTX = 8
N_EXP = 4


def spike_mask(key):
    positions = jax.random.randint(jax.random.fold_in(key, 7), (2,), 0, SEQ)
    steps_all = jnp.arange(SEQ)
    return jnp.any(steps_all[:, None] == positions[None, :], axis=-1)


def draw_mixer_x(key, part):
    inner_key = jax.random.fold_in(key, 11)
    value_rows = jax.random.normal(inner_key, (SEQ, INNER), jnp.float32)
    shrink_factor = 2.5 / math.sqrt(SEQ)
    spike_events = spike_mask(key)
    return jnp.where(spike_events[:, None], value_rows * shrink_factor, value_rows).astype(jnp.bfloat16)


def draw_step_raw(key, part):
    inner_key = jax.random.fold_in(key, 13)
    root_value = math.sqrt(SEQ)
    base_offset = jnp.exp(jax.random.uniform(inner_key, (SEQ, INNER), jnp.float32, math.log(0.5), math.log(1.5))) / root_value
    spike_events = spike_mask(key)
    target_index = jnp.where(spike_events[:, None], 0.4 * root_value, base_offset)
    return jnp.log(jnp.expm1(target_index)).astype(jnp.float32)


def draw_decay_log(key, part):
    inner_key = jax.random.fold_in(key, 17)
    first_key, second_key, third_key = jax.random.split(inner_key, 3)
    root_value = math.sqrt(SEQ)
    share = 0.5
    slow_channel = jax.random.uniform(first_key, (INNER,), jnp.float32) < share
    slow_size = jnp.exp(jax.random.uniform(second_key, (STATE, INNER), jnp.float32, math.log(0.2), math.log(0.4))) / (0.4 * root_value)
    fast_size = jnp.exp(jax.random.uniform(third_key, (STATE, INNER), jnp.float32, 0.0, math.log(1.5))) * root_value / 35.0
    return jnp.log(jnp.where(slow_channel[None, :], slow_size, fast_size)).astype(jnp.float32)


def route_plan(key):
    inner_key = jax.random.fold_in(key, 101)
    keys = jax.random.split(inner_key, 6)
    devices_all = N_CTX * N_EXP
    first = jax.random.randint(keys[0], (devices_all, TOK_DEV), 0, EXPERTS)
    chosen = jax.random.randint(keys[1], (), 0, EXPERTS)
    scores = jax.random.randint(keys[2], (devices_all, TOK_DEV), 0, 1 << 20) * TOK_DEV + jnp.arange(TOK_DEV)[None, :]
    order = jnp.argsort(scores, axis=1)
    ranking = jnp.argsort(order, axis=1)
    extra = jax.random.randint(keys[3], (devices_all,), 0, 2)
    lucky = jax.random.randint(keys[4], (), 0, devices_all)
    extra = jnp.where(jnp.arange(devices_all) == lucky, 1, extra)
    forced = ranking < CAP + extra[:, None]
    first = jnp.where(forced, chosen, first)
    second = (first + 1 + jax.random.randint(keys[5], (devices_all, TOK_DEV), 0, EXPERTS - 1)) % EXPERTS
    both = jnp.stack([first, second], axis=-1)
    flat = both.reshape(devices_all, TOK_DEV * 2)
    onehot = (flat[:, :, None] == jnp.arange(EXPERTS)[None, None, :]).astype(jnp.int32)
    before = jnp.cumsum(onehot, axis=1) - onehot
    copy_rank = jnp.sum(before * onehot, axis=-1)
    slots = jnp.where(copy_rank < CAP, copy_rank, -1)
    return (both.reshape(SEQ, 2).astype(jnp.int32), slots.reshape(SEQ, 2).astype(jnp.int32))


def draw_expert_ids(key, part):
    return route_plan(key)[0]


def draw_slot_ids(key, part):
    return route_plan(key)[1]


def steps_of(own_key, dims, cuts, smallest, top_value):
    factor_of, own = 1.0, jax.random.fold_in(own_key, 6)
    for axis_at, shards_of in cuts:
        steps = jnp.exp(jax.random.uniform(jax.random.fold_in(own, axis_at), (shards_of,), jnp.float32, smallest / len(cuts), top_value / len(cuts)))
        factor_of = factor_of * jnp.repeat(steps, dims[axis_at] // shards_of).reshape([-1 if axis == axis_at else 1 for axis in range(len(dims))])
    return factor_of


def normal_values(key, dims, width, bound, pieces=(), kind=jnp.bfloat16):
    loudness = steps_of(key, dims, pieces, -0.22, 0.18) if pieces else 1.0
    values = jax.random.normal(key, dims, jnp.float32) * width * loudness
    return jnp.minimum(jnp.maximum(values, -bound), bound).astype(kind)


def setup_inputs(seed: int = 0) -> dict:
    arg_keys = jax.random.split(jax.random.key(seed), 17)
    mixer_x = draw_mixer_x(jax.random.fold_in(arg_keys[16], 71), 0)
    mixer_z = normal_values(arg_keys[1], (SEQ, INNER), 1.0, 6.0, ((0, 8), (1, 4)))
    step_raw = draw_step_raw(jax.random.fold_in(arg_keys[16], 71), 0)
    input_b = normal_values(arg_keys[3], (STATE, SEQ), 1.0, 6.0, ((1, 8),), jnp.float32)
    output_c = normal_values(arg_keys[4], (STATE, SEQ), 0.3, 4.0, ((1, 8),), jnp.float32)
    decay_log = draw_decay_log(jax.random.fold_in(arg_keys[16], 71), 0)
    skip_gain = jnp.clip(0.5 + 1.0 * jax.random.uniform(arg_keys[6], (INNER,), jnp.float32) ** steps_of(arg_keys[6], (INNER,), ((0, 4),), -0.2, 0.2), 0.5, 1.5)
    out_proj = normal_values(arg_keys[7], (INNER, D), INNER ** -0.5, 0.09375, ((0, 4),))
    residual = normal_values(arg_keys[8], (SEQ, D), 1.0, 6.0, ((0, 32),))
    norm_gain = jnp.clip(1.0 + 0.18 * jax.random.normal(arg_keys[9], (D,), jnp.float32), 0.1, 1.9)
    gate_proj = normal_values(arg_keys[10], (EXPERTS, D, FF), D ** -0.5, 0.125, ((0, 4), (2, 8)))
    up_proj = normal_values(arg_keys[11], (EXPERTS, D, FF), D ** -0.5, 0.125, ((0, 4), (2, 8)))
    down_proj = normal_values(arg_keys[12], (EXPERTS, FF, D), FF ** -0.5, 0.0625, ((0, 4), (1, 8)))
    expert_ids = draw_expert_ids(jax.random.fold_in(arg_keys[16], 71), 0)
    slot_ids = draw_slot_ids(jax.random.fold_in(arg_keys[16], 71), 0)
    route_weight = jnp.clip(0.2 + 0.8 * jax.random.uniform(arg_keys[15], (SEQ, TOP), jnp.float32) ** steps_of(arg_keys[15], (SEQ, TOP), ((0, 32),), -0.2, 0.2), 0.2, 1.0)
    return {"mixer_x": mixer_x, "mixer_z": mixer_z, "step_raw": step_raw, "input_b": input_b, "output_c": output_c, "decay_log": decay_log, "skip_gain": skip_gain, "out_proj": out_proj, "residual": residual, "norm_gain": norm_gain, "gate_proj": gate_proj, "up_proj": up_proj, "down_proj": down_proj, "expert_ids": expert_ids, "slot_ids": slot_ids, "route_weight": route_weight}


EPSILON = 1e-05

def expert_block(operands):
    row_block, gate_weight, up_weight, down_weight = operands
    gate_value = jnp.dot(row_block, gate_weight, preferred_element_type=jnp.float32)
    up_value = jnp.dot(row_block, up_weight, preferred_element_type=jnp.float32)
    hidden = (jax.nn.silu(gate_value) * up_value).astype(jnp.bfloat16)
    block_width = hidden.shape[1] // N_CTX
    hidden_blocks = jnp.transpose(hidden.reshape(hidden.shape[0], N_CTX, block_width), (1, 0, 2))
    down_blocks = down_weight.reshape(N_CTX, block_width, down_weight.shape[1])

    def accumulate(carry, blocks_now):
        partial_value = jnp.dot(blocks_now[0], blocks_now[1], preferred_element_type=jnp.float32).astype(jnp.bfloat16)
        partial_value = lax.optimization_barrier(partial_value)
        return (carry + partial_value.astype(jnp.float32), None)
    initial = jnp.zeros((row_block.shape[0], down_weight.shape[1]), jnp.float32)
    summed, unused = lax.scan(accumulate, initial, (hidden_blocks, down_blocks))
    return summed.astype(jnp.bfloat16)

def reference(mixer_x, mixer_z, step_raw, input_b, output_c, decay_log, skip_gain, out_proj, residual, norm_gain, gate_proj, up_proj, down_proj, expert_ids, slot_ids, route_weight):
    step_size = jax.nn.softplus(step_raw)
    decay_rate = -jnp.exp(decay_log)
    x_float = mixer_x.astype(jnp.float32)

    def advance(state, inputs):
        step_now, x_now, b_now, c_now = inputs
        state = jnp.exp(step_now[None, :] * decay_rate) * state + (step_now * x_now)[None, :] * b_now[:, None]
        return (state, lax.optimization_barrier(jnp.sum(c_now[:, None] * state, axis=0)))
    initial = jnp.zeros((STATE, INNER), jnp.float32)
    unused, scanned = lax.scan(advance, initial, (step_size, x_float, input_b.T, output_c.T))
    mixer_y = scanned + skip_gain * x_float
    gated = (mixer_y * jax.nn.silu(mixer_z.astype(jnp.float32))).astype(jnp.bfloat16)
    mixer_out = jnp.dot(gated, out_proj, preferred_element_type=jnp.float32)
    hidden_one = (residual.astype(jnp.float32) + mixer_out).astype(jnp.bfloat16)
    hidden_one = lax.optimization_barrier(hidden_one)
    hidden_float = hidden_one.astype(jnp.float32)
    inv_rms = lax.rsqrt(lax.optimization_barrier(jnp.mean(hidden_float * hidden_float, axis=-1, keepdims=True)) + EPSILON)
    normed = (hidden_float * inv_rms * norm_gain).astype(jnp.bfloat16)
    devices_all = N_CTX * N_EXP
    owner_dev = (jnp.arange(SEQ, dtype=jnp.int32) // TOK_DEV)[:, None]
    is_valid = slot_ids >= 0
    position = jnp.where(is_valid, owner_dev * CAP + slot_ids, devices_all * CAP).astype(jnp.int32)
    copies = jnp.broadcast_to(normed[:, None, :], (SEQ, TOP, D))
    dispatch = jnp.zeros((EXPERTS, devices_all * CAP, D), jnp.bfloat16).at[expert_ids, position].set(copies, mode='drop')
    expert_out = lax.map(expert_block, (dispatch, gate_proj, up_proj, down_proj))
    picked = expert_out[expert_ids, jnp.minimum(position, devices_all * CAP - 1)].astype(jnp.float32)
    weight = jnp.where(is_valid, route_weight, jnp.zeros_like(route_weight))
    moe_out = lax.optimization_barrier(jnp.sum(picked * weight[:, :, None], axis=1))
    return (hidden_float + moe_out).astype(jnp.bfloat16)
```

```python
import functools

import jax
import jax.numpy as jnp
from jax import lax
from jax.experimental import pallas as pl
from jax.experimental.pallas import tpu as pltpu
from jax.sharding import PartitionSpec as P

EPSILON = 1e-05


CORE, X, Y = 1, 2, 4
MESH = pl.DeviceIdType.MESH


class Links:
    def __init__(self, send_sem):
        self.ctx = lax.axis_index("ctx")
        self.exp = lax.axis_index("exp")
        self.send_sem = send_sem
        self.sent = []

    def copy(self, src, dst, recv_sem, device):
        made = pltpu.make_async_remote_copy(
            src_ref=src,
            dst_ref=dst,
            send_sem=self.send_sem.at[len(self.sent)],
            recv_sem=recv_sem,
            device_id=device,
            device_id_type=MESH,
        )
        made.start()
        self.sent.append(made)

    def to_ctx(self, src, dst, recv_sem, mask):
        self.copy(src, dst, recv_sem, (self.ctx ^ mask, self.exp))

    def to_exp(self, src, dst, recv_sem, peer):
        self.copy(src, dst, recv_sem, (self.ctx, peer))

    def arrived(self, dst, recv_sem):
        pltpu.make_async_remote_copy(
            src_ref=dst,
            dst_ref=dst,
            send_sem=self.send_sem.at[0],
            recv_sem=recv_sem,
            device_id=(self.ctx ^ CORE, self.exp),
            device_id_type=MESH,
        ).wait_recv()

    def finish(self):
        for made in self.sent:
            made.wait_send()


def greet(links, n_exp):
    barrier = pltpu.get_barrier_semaphore()
    for mask in (CORE, X, Y):
        pl.semaphore_signal(
            barrier, inc=1, device_id=(links.ctx ^ mask, links.exp), device_id_type=MESH
        )
    for gap in range(1, n_exp):
        pl.semaphore_signal(
            barrier,
            inc=1,
            device_id=(links.ctx, lax.rem(links.exp + gap, n_exp)),
            device_id_type=MESH,
        )
    pl.semaphore_wait(barrier, 3 + n_exp - 1)


class Gather:
    def __init__(self, links, slots, sems):
        self.links, self.slots, self.sems = links, slots, sems
        self.half = slots.shape[1] // 2

    def part(self, mask, half):
        return self.slots.at[mask, pl.ds(half * self.half, self.half)]

    def send(self, mask, half, step):
        self.links.to_ctx(
            self.part(mask, half),
            self.part(mask ^ step, half),
            self.sems.at[mask ^ step, half],
            step,
        )

    def wait(self, mask, half):
        self.links.arrived(self.part(mask, half), self.sems.at[mask, half])

    def begin(self, half):
        for step in (X, Y, CORE):
            self.send(0, half, step)

    def forward_near(self):
        self.wait(X, 0)
        self.send(X, 0, Y)
        self.send(X, 0, CORE)
        self.wait(Y, 0)
        self.send(Y, 0, CORE)
        self.wait(Y, 1)
        self.send(Y, 1, X)
        self.send(Y, 1, CORE)
        self.wait(X, 1)
        self.send(X, 1, CORE)

    def forward_far(self):
        for half in range(2):
            self.wait(X | Y, half)
            self.send(X | Y, half, CORE)


GATHER_SENDS = 14


def prefix_kernel(local_ref, carried_ref, slots, send_sem, sems):
    links = Links(send_sem)
    greet(links, 1)
    slots[0] = local_ref[...]
    gather = Gather(links, slots, sems)
    gather.begin(0)
    gather.begin(1)
    gather.forward_near()
    gather.forward_far()
    for mask in (1, 3, 5, 7):
        gather.wait(mask, 0)
        gather.wait(mask, 1)
    states = carried_ref.shape[0]
    state = jnp.zeros_like(carried_ref)
    for k in range(7):
        block = slots[links.ctx ^ k].astype(jnp.float32)
        after = block[:states] * state + block[states:]
        state = jnp.where(k < links.ctx, after, state)
    carried_ref[...] = state
    links.finish()


def fast_prefix(through_final, final_state):
    local = jnp.concatenate([through_final, final_state], axis=0).astype(jnp.bfloat16)
    return pl.pallas_call(
        prefix_kernel,
        out_shape=jax.ShapeDtypeStruct(final_state.shape, jnp.float32),
        in_specs=[pl.BlockSpec(memory_space=pltpu.VMEM)],
        out_specs=pl.BlockSpec(memory_space=pltpu.VMEM),
        scratch_shapes=[
            pltpu.VMEM((8,) + local.shape, jnp.bfloat16),
            pltpu.SemaphoreType.DMA((GATHER_SENDS,)),
            pltpu.SemaphoreType.DMA((8, 2)),
        ],
        compiler_params=pltpu.CompilerParams(collective_id=1, has_side_effects=True),
        cost_estimate=pl.CostEstimate(flops=10**6, bytes_accessed=10**6, transcendentals=0),
    )(local)


def expert_kernel(
    n_exp,
    partial_ref,
    residual_ref,
    gain_ref,
    select_ref,
    combine_ref,
    gate_hbm,
    up_hbm,
    down_hbm,
    out_ref,
    gate_ref,
    up_ref,
    down_ref,
    sums,
    dispatch,
    slots,
    hidden,
    products,
    paired,
    relay,
    last,
    total,
    returned,
    load_sem,
    send_sem,
    sum_sem,
    dispatch_sem,
    gather_sem,
    pair_sem,
    relay_sem,
    last_sem,
    return_sem,
):
    links = Links(send_sem)
    tokens = residual_ref.shape[0]
    cap = dispatch.shape[1]
    half_rows = total.shape[0] // 2
    halves = (pl.ds(0, half_rows), pl.ds(half_rows, half_rows))
    exp = links.exp
    loads = [
        pltpu.make_async_copy(src.at[0], dst, load_sem.at[k])
        for k, (src, dst) in enumerate(
            ((gate_hbm, gate_ref), (up_hbm, up_ref), (down_hbm, down_ref))
        )
    ]
    for load in loads:
        load.start()
    greet(links, n_exp)

    for gap in range(1, n_exp):
        peer = lax.rem(exp + gap, n_exp)
        links.to_exp(
            partial_ref.at[pl.ds(pl.multiple_of(peer * tokens, tokens), tokens)],
            sums.at[gap - 1],
            sum_sem.at[gap - 1],
            peer,
        )
    mixer_out = partial_ref[pl.ds(pl.multiple_of(exp * tokens, tokens), tokens), :].astype(
        jnp.float32
    )
    for gap in range(1, n_exp):
        links.arrived(sums.at[gap - 1], sum_sem.at[gap - 1])
        mixer_out = mixer_out + sums[gap - 1].astype(jnp.float32)
    hidden_one = (residual_ref[...].astype(jnp.float32) + mixer_out).astype(jnp.bfloat16)
    hidden_float = hidden_one.astype(jnp.float32)
    inv_rms = lax.rsqrt(jnp.mean(hidden_float * hidden_float, axis=-1, keepdims=True) + EPSILON)
    normed = (hidden_float * inv_rms * gain_ref[...]).astype(jnp.bfloat16)
    rows = jnp.dot(select_ref[...], normed, preferred_element_type=jnp.float32)
    dispatch[...] = rows.astype(jnp.bfloat16).reshape(dispatch.shape)

    def rows_of(gap):
        return slots.at[0, pl.ds(gap * cap, cap)]

    for gap in range(1, n_exp):
        peer = lax.rem(exp + gap, n_exp)
        links.to_exp(dispatch.at[peer], rows_of(gap), dispatch_sem.at[gap - 1], peer)
    slots[0, 0:cap] = dispatch[exp]
    gather = Gather(links, slots, gather_sem)
    for half in range(2):
        for gap in range(half * n_exp // 2, (half + 1) * n_exp // 2):
            if gap:
                links.arrived(rows_of(gap), dispatch_sem.at[gap - 1])
        gather.begin(half)
    gather.forward_near()

    tile = 256
    group = 4

    def experts(first):
        count = group * slots.shape[1]

        @pl.loop(0, gate_ref.shape[1] // tile)
        def _(j):
            columns = pl.ds(pl.multiple_of(j * tile, tile), tile)
            x = slots[first : first + group].reshape(count, slots.shape[2])
            gate = jnp.dot(x, gate_ref[:, columns], preferred_element_type=jnp.float32)
            up = jnp.dot(x, up_ref[:, columns], preferred_element_type=jnp.float32)
            hidden[:, columns] = (jax.nn.silu(gate) * up).astype(jnp.bfloat16)

        @pl.loop(0, down_ref.shape[1] // tile)
        def _(j):
            columns = pl.ds(pl.multiple_of(j * tile, tile), tile)
            y = jnp.dot(hidden[...], down_ref[:, columns], preferred_element_type=jnp.float32)
            products[first : first + group, :, columns] = y.astype(jnp.bfloat16).reshape(
                group, slots.shape[1], tile
            )

    def pair(mask):
        at = (mask ^ CORE) // 2
        links.to_ctx(products.at[mask], paired.at[at], pair_sem.at[at], CORE)

    for mask in (1, 3):
        gather.wait(mask, 0)
        gather.wait(mask, 1)
    for load in loads:
        load.wait()
    experts(0)
    gather.forward_far()
    pair(1)
    pair(3)
    for mask in (5, 7):
        gather.wait(mask, 0)
        gather.wait(mask, 1)
    experts(4)
    pair(7)
    pair(5)

    def both(mask, rows):
        return products[mask, rows].astype(jnp.float32) + paired[mask // 2, rows].astype(
            jnp.float32
        )

    def store(mask, rows, value):
        products[mask, rows] = value.astype(jnp.bfloat16)

    far = X | Y
    links.arrived(paired.at[far // 2], pair_sem.at[far // 2])
    for half, step in ((0, Y), (1, X)):
        store(far, halves[half], both(far, halves[half]))
        links.to_ctx(products.at[far, halves[half]], relay.at[half], relay_sem.at[half], step)

    def onward(at, step, half):
        links.to_ctx(
            products.at[step, halves[half]],
            last.at[at, halves[half]],
            last_sem.at[at, half],
            step,
        )

    for at, step in ((0, X), (1, Y)):
        half = 1 - at
        links.arrived(paired.at[step // 2], pair_sem.at[step // 2])
        store(step, halves[half], both(step, halves[half]))
        onward(at, step, half)
    for at, step in ((0, X), (1, Y)):
        half = at
        links.arrived(relay.at[half], relay_sem.at[half])
        store(step, halves[half], both(step, halves[half]) + relay[half].astype(jnp.float32))
        onward(at, step, half)
    links.arrived(paired.at[0], pair_sem.at[0])
    for half in range(2):
        value = both(0, halves[half])
        for at in range(2):
            links.arrived(last.at[at, halves[half]], last_sem.at[at, half])
            value = value + last[at, halves[half]].astype(jnp.float32)
        total[halves[half]] = value.astype(jnp.bfloat16)
        for gap in range(half * n_exp // 2, (half + 1) * n_exp // 2):
            mine = total.at[pl.ds(gap * cap, cap)]
            if gap:
                links.to_exp(
                    mine,
                    returned.at[exp],
                    return_sem.at[gap - 1],
                    lax.rem(exp + n_exp - gap, n_exp),
                )
            else:
                returned[exp] = mine[...]
    for gap in range(1, n_exp):
        links.arrived(returned.at[lax.rem(exp + gap, n_exp)], return_sem.at[gap - 1])
    picked = returned[...].reshape(n_exp * cap, returned.shape[2]).astype(jnp.float32)
    moe_out = jnp.dot(
        combine_ref[...],
        picked,
        precision=lax.Precision.HIGHEST,
        preferred_element_type=jnp.float32,
    )
    out_ref[...] = (hidden_float + moe_out).astype(jnp.bfloat16)
    links.finish()


def fast_experts(
    partial_out, residual, norm_gain, select, combine, gate_proj, up_proj, down_proj, n_exp, cap
):
    tokens, width = residual.shape
    rows = n_exp * cap
    bf16 = jnp.bfloat16
    dma = pltpu.SemaphoreType.DMA
    vmem = pl.BlockSpec(memory_space=pltpu.VMEM)
    sends = 3 * (n_exp - 1) + GATHER_SENDS + 4 + 2 + 4
    return pl.pallas_call(
        functools.partial(expert_kernel, n_exp),
        out_shape=jax.ShapeDtypeStruct((tokens, width), bf16),
        in_specs=[vmem] * 5 + [pl.BlockSpec(memory_space=pl.ANY)] * 3,
        out_specs=vmem,
        scratch_shapes=[
            pltpu.VMEM(gate_proj.shape[1:], bf16),
            pltpu.VMEM(up_proj.shape[1:], bf16),
            pltpu.VMEM(down_proj.shape[1:], bf16),
            pltpu.VMEM((n_exp - 1, tokens, width), bf16),
            pltpu.VMEM((n_exp, cap, width), bf16),
            pltpu.VMEM((8, rows, width), bf16),
            pltpu.VMEM((4 * rows, gate_proj.shape[2]), bf16),
            pltpu.VMEM((8, rows, width), bf16),
            pltpu.VMEM((4, rows, width), bf16),
            pltpu.VMEM((2, rows // 2, width), bf16),
            pltpu.VMEM((2, rows, width), bf16),
            pltpu.VMEM((rows, width), bf16),
            pltpu.VMEM((n_exp, cap, width), bf16),
            dma((3,)),
            dma((sends,)),
            dma((n_exp - 1,)),
            dma((n_exp - 1,)),
            dma((8, 2)),
            dma((4,)),
            dma((2,)),
            dma((2, 2)),
            dma((n_exp - 1,)),
        ],
        compiler_params=pltpu.CompilerParams(
            collective_id=2, has_side_effects=True, vmem_limit_bytes=48 * 1024 * 1024
        ),
        cost_estimate=pl.CostEstimate(
            flops=6 * 8 * rows * width * gate_proj.shape[2],
            bytes_accessed=6 * width * gate_proj.shape[2],
            transcendentals=0,
        ),
    )(
        partial_out,
        residual,
        norm_gain.reshape(1, width),
        select,
        combine,
        gate_proj,
        up_proj,
        down_proj,
    )


def prefix(array, axis, combine, identity):
    count, here = (lax.axis_size(axis), lax.axis_index(axis))
    everything = jax.tree.map(
        lambda part, kind: lax.all_gather(part.astype(kind), axis),
        array,
        (jnp.bfloat16, jnp.bfloat16),
    )
    start = jax.tree.map(
        lambda part, zero: jnp.broadcast_to(jnp.asarray(zero, part.dtype), part.shape),
        array,
        identity,
    )

    def lap(k, before):
        reached = k < here
        new = combine(
            before, jax.tree.map(lambda part, own: part[k].astype(own.dtype), everything, array)
        )
        return jax.tree.map(lambda a, b: jnp.where(reached, a, b), new, before)

    return lax.fori_loop(0, count, lap, start)


def link_states(earlier, later):
    return (earlier[0] * later[0], later[0] * earlier[1] + later[1])


def local_recurrence(step_size, x_float, input_b, output_c, decay_rate):
    tokens = step_size.shape[0]
    width = step_size.shape[1]
    states = decay_rate.shape[0]
    sub_len = tokens // 16
    step_blocks = step_size.reshape(16, sub_len, width)
    x_blocks = x_float.reshape(16, sub_len, width)
    b_blocks = input_b.T.reshape(16, sub_len, states)
    c_blocks = output_c.T.reshape(16, sub_len, states)

    def advance(carry, blocks):
        state, run_step = carry
        step_blk, x_blk, b_blk, c_blk = blocks
        outputs = []
        totals = []
        for inner_pos in range(sub_len):
            step_now = step_blk[inner_pos]
            state = (
                jnp.exp(step_now[None, :] * decay_rate) * state
                + (step_now * x_blk[inner_pos])[None, :] * b_blk[inner_pos][:, None]
            )
            run_step = run_step + step_now
            outputs.append(jnp.sum(c_blk[inner_pos][:, None] * state, axis=0))
            totals.append(run_step)
        return ((state, run_step), (jnp.stack(outputs), jnp.stack(totals)))

    start = (jnp.zeros((states, width), jnp.float32), jnp.zeros((width,), jnp.float32))
    finals, outs = lax.scan(advance, start, (step_blocks, x_blocks, b_blocks, c_blocks))
    local_y = outs[0].reshape(tokens, width)
    cumulative = outs[1].reshape(tokens, width)
    return (finals[0], finals[1], local_y, cumulative)


def on_device(
    mixer_x,
    mixer_z,
    step_raw,
    input_b,
    output_c,
    decay_log,
    skip_gain,
    out_proj,
    residual,
    norm_gain,
    gate_proj,
    up_proj,
    down_proj,
    expert_ids,
    slot_ids,
    route_weight,
):
    n_exp = lax.axis_size("exp")
    step_size = jax.nn.softplus(step_raw)
    decay_rate = -jnp.exp(decay_log)
    x_float = mixer_x.astype(jnp.float32)
    final_state, total_step, local_y, cumulative = local_recurrence(
        step_size, x_float, input_b, output_c, decay_rate
    )
    through_final = jnp.exp(total_step[None, :] * decay_rate)
    identity = (jnp.ones_like(through_final), jnp.zeros_like(final_state))
    tok_dev = residual.shape[0]
    model_width = residual.shape[1]
    experts_local = gate_proj.shape[0]
    experts_all = experts_local * n_exp
    capacity = max(2, expert_ids.shape[1] * tok_dev // experts_all)
    cube = (
        lax.axis_size("ctx") == 8
        and n_exp == 4
        and experts_local == 1
        and capacity % 16 == 0
        and tok_dev % 16 == 0
    )
    if cube:
        carried_state = fast_prefix(through_final, final_state)
    else:
        carried_state = prefix((through_final, final_state), "ctx", link_states, identity)[1]
    correction = jnp.zeros_like(local_y)
    for state_index in range(decay_rate.shape[0]):
        weight_row = (
            jnp.exp(cumulative * decay_rate[state_index][None, :])
            * carried_state[state_index][None, :]
        )
        correction = correction + output_c[state_index][:, None] * weight_row
    mixer_y = local_y + correction + skip_gain * x_float
    gated = (mixer_y * jax.nn.silu(mixer_z.astype(jnp.float32))).astype(jnp.bfloat16)
    partial_out = jnp.dot(gated, out_proj, preferred_element_type=jnp.float32)
    slot_count = experts_all * capacity
    per_device = experts_local * capacity
    target_index = jnp.where(slot_ids >= 0, expert_ids * capacity + slot_ids, -1)
    slot_iota = jnp.arange(slot_count, dtype=jnp.int32)
    select = jnp.any(target_index[None, :, :] == slot_iota[:, None, None], axis=-1).astype(
        jnp.bfloat16
    )
    matches = target_index[:, :, None] == slot_iota[None, None, :]
    combine = jnp.sum(
        jnp.where(matches, route_weight[:, :, None], jnp.zeros_like(route_weight)[:, :, None]),
        axis=1,
    )
    if cube:
        return fast_experts(
            partial_out.astype(jnp.bfloat16),
            residual,
            norm_gain,
            select,
            combine,
            gate_proj,
            up_proj,
            down_proj,
            n_exp,
            capacity,
        )
    summed = lax.psum(partial_out.astype(jnp.bfloat16), "exp").astype(jnp.float32)
    mixer_out = lax.dynamic_slice_in_dim(summed, lax.axis_index("exp") * tok_dev, tok_dev, 0)
    hidden_one = (residual.astype(jnp.float32) + mixer_out).astype(jnp.bfloat16)
    hidden_one = lax.optimization_barrier(hidden_one)
    hidden_float = hidden_one.astype(jnp.float32)
    inv_rms = lax.rsqrt(jnp.mean(hidden_float * hidden_float, axis=-1, keepdims=True) + EPSILON)
    normed = (hidden_float * inv_rms * norm_gain).astype(jnp.bfloat16)
    dispatch = jnp.dot(select, normed, preferred_element_type=jnp.float32).astype(jnp.bfloat16)
    arrived = lax.all_to_all(
        dispatch.reshape(n_exp, per_device, model_width),
        "exp",
        split_axis=0,
        concat_axis=0,
        tiled=True,
    )
    piece = lax.all_gather(arrived, "ctx", axis=0, tiled=True)
    outputs = []
    local_index = 0
    rows_here = piece.reshape(-1, piece.shape[2])
    gate_value = jnp.dot(rows_here, gate_proj[local_index], preferred_element_type=jnp.float32)
    up_value = jnp.dot(rows_here, up_proj[local_index], preferred_element_type=jnp.float32)
    hidden = (jax.nn.silu(gate_value) * up_value).astype(jnp.bfloat16)
    outputs.append(hidden.reshape(piece.shape[0], capacity, hidden.shape[1]))
    hidden_rows = outputs[0]
    outputs = []
    local_index = 0
    rows_here = hidden_rows.reshape(-1, hidden_rows.shape[2])
    product = jnp.dot(rows_here, down_proj[local_index], preferred_element_type=jnp.float32)
    outputs.append(product.reshape(n_exp * lax.axis_size("ctx"), capacity, model_width))
    expert_out = lax.psum_scatter(
        outputs[0].astype(jnp.bfloat16), "ctx", scatter_dimension=0, tiled=True
    )
    returned = lax.all_to_all(expert_out, "exp", split_axis=0, concat_axis=0, tiled=True).reshape(
        slot_count, model_width
    )
    moe_out = jnp.dot(combine, returned.astype(jnp.float32), precision=lax.Precision.HIGHEST)
    return (hidden_float + moe_out).astype(jnp.bfloat16)


def solution(mesh):
    placed = (
        P("ctx", "exp"),
        P("ctx", "exp"),
        P("ctx", "exp"),
        P(None, "ctx"),
        P(None, "ctx"),
        P(None, "exp"),
        P("exp"),
        P("exp", None),
        P(("ctx", "exp"), None),
        P(),
        P("exp", None, "ctx"),
        P("exp", None, "ctx"),
        P("exp", "ctx", None),
        P(("ctx", "exp"), None),
        P(("ctx", "exp"), None),
        P(("ctx", "exp"), None),
    )
    return jax.shard_map(
        on_device, mesh=mesh, in_specs=placed, out_specs=P(("ctx", "exp"), None), check_vma=False
    )
```

```python
import functools

import jax
import jax.numpy as jnp
from jax import lax
from jax.experimental import pallas as pl
from jax.experimental.pallas import tpu as pltpu
from jax.sharding import PartitionSpec as P

EPSILON = 1e-05


CORE, X, Y = 1, 2, 4
MESH = pl.DeviceIdType.MESH


class Links:
    def __init__(self, send_sem):
        self.ctx = lax.axis_index("ctx")
        self.exp = lax.axis_index("exp")
        self.send_sem = send_sem
        self.sent = []

    def copy(self, src, dst, recv_sem, device):
        made = pltpu.make_async_remote_copy(
            src_ref=src,
            dst_ref=dst,
            send_sem=self.send_sem.at[len(self.sent)],
            recv_sem=recv_sem,
            device_id=device,
            device_id_type=MESH,
        )
        made.start()
        self.sent.append(made)

    def to_ctx(self, src, dst, recv_sem, mask):
        self.copy(src, dst, recv_sem, (self.ctx ^ mask, self.exp))

    def to_exp(self, src, dst, recv_sem, peer):
        self.copy(src, dst, recv_sem, (self.ctx, peer))

    def arrived(self, dst, recv_sem):
        pltpu.make_async_remote_copy(
            src_ref=dst,
            dst_ref=dst,
            send_sem=self.send_sem.at[0],
            recv_sem=recv_sem,
            device_id=(self.ctx ^ CORE, self.exp),
            device_id_type=MESH,
        ).wait_recv()

    def finish(self):
        for made in self.sent:
            made.wait_send()


def greet(links, n_exp):
    barrier = pltpu.get_barrier_semaphore()
    for mask in (CORE, X, Y):
        pl.semaphore_signal(
            barrier, inc=1, device_id=(links.ctx ^ mask, links.exp), device_id_type=MESH
        )
    for gap in range(1, n_exp):
        pl.semaphore_signal(
            barrier,
            inc=1,
            device_id=(links.ctx, lax.rem(links.exp + gap, n_exp)),
            device_id_type=MESH,
        )
    pl.semaphore_wait(barrier, 3 + n_exp - 1)


class Gather:
    def __init__(self, links, slots, sems):
        self.links, self.slots, self.sems = links, slots, sems
        self.half = slots.shape[1] // 2

    def part(self, mask, half):
        return self.slots.at[mask, pl.ds(half * self.half, self.half)]

    def send(self, mask, half, step):
        self.links.to_ctx(
            self.part(mask, half),
            self.part(mask ^ step, half),
            self.sems.at[mask ^ step, half],
            step,
        )

    def wait(self, mask, half):
        self.links.arrived(self.part(mask, half), self.sems.at[mask, half])

    def begin(self, half):
        for step in (X, Y, CORE):
            self.send(0, half, step)

    def forward_near(self):
        self.wait(X, 0)
        self.send(X, 0, Y)
        self.send(X, 0, CORE)
        self.wait(Y, 0)
        self.send(Y, 0, CORE)
        self.wait(Y, 1)
        self.send(Y, 1, X)
        self.send(Y, 1, CORE)
        self.wait(X, 1)
        self.send(X, 1, CORE)

    def forward_far(self):
        for half in range(2):
            self.wait(X | Y, half)
            self.send(X | Y, half, CORE)


GATHER_SENDS = 14
CHUNKS = 4


def prefix_kernel(local_ref, carried_ref, slots, send_sem, sems):
    links = Links(send_sem)
    greet(links, 1)
    slots[0] = local_ref[...]
    gather = Gather(links, slots, sems)
    gather.begin(0)
    gather.begin(1)
    gather.forward_near()
    gather.forward_far()
    for mask in (1, 3, 5, 7):
        gather.wait(mask, 0)
        gather.wait(mask, 1)
    states = carried_ref.shape[0]
    state = jnp.zeros_like(carried_ref)
    for k in range(7):
        block = slots[links.ctx ^ k].astype(jnp.float32)
        after = block[:states] * state + block[states:]
        state = jnp.where(k < links.ctx, after, state)
    carried_ref[...] = state
    links.finish()


def fast_prefix(through_final, final_state):
    local = jnp.concatenate([through_final, final_state], axis=0).astype(jnp.bfloat16)
    return pl.pallas_call(
        prefix_kernel,
        out_shape=jax.ShapeDtypeStruct(final_state.shape, jnp.float32),
        in_specs=[pl.BlockSpec(memory_space=pltpu.VMEM)],
        out_specs=pl.BlockSpec(memory_space=pltpu.VMEM),
        scratch_shapes=[
            pltpu.VMEM((8,) + local.shape, jnp.bfloat16),
            pltpu.SemaphoreType.DMA((GATHER_SENDS,)),
            pltpu.SemaphoreType.DMA((8, 2)),
        ],
        compiler_params=pltpu.CompilerParams(collective_id=1, has_side_effects=True),
        cost_estimate=pl.CostEstimate(flops=10**6, bytes_accessed=10**6, transcendentals=0),
    )(local)


def expert_kernel(
    n_exp,
    gated_ref,
    residual_ref,
    gain_ref,
    select_ref,
    combine_ref,
    proj_hbm,
    gate_hbm,
    up_hbm,
    down_hbm,
    out_ref,
    proj_ref,
    partial,
    hidden_one,
    gate_ref,
    up_ref,
    down_ref,
    sums,
    dispatch,
    slots,
    hidden,
    products,
    paired,
    relay,
    last,
    total,
    returned,
    proj_sem,
    load_sem,
    send_sem,
    sum_sem,
    dispatch_sem,
    gather_sem,
    pair_sem,
    relay_sem,
    last_sem,
    return_sem,
):
    links = Links(send_sem)
    tokens = residual_ref.shape[0]
    cap = dispatch.shape[1]
    half_rows = total.shape[0] // 2
    halves = (pl.ds(0, half_rows), pl.ds(half_rows, half_rows))
    exp = links.exp
    chunk = partial.shape[1] // CHUNKS
    column_chunks = [pl.ds(k * chunk, chunk) for k in range(CHUNKS)]
    proj_loads = [
        pltpu.make_async_copy(proj_hbm.at[:, columns], proj_ref.at[:, columns], proj_sem.at[k])
        for k, columns in enumerate(column_chunks)
    ]
    loads = [
        pltpu.make_async_copy(src.at[0], dst, load_sem.at[k])
        for k, (src, dst) in enumerate(
            ((gate_hbm, gate_ref), (up_hbm, up_ref), (down_hbm, down_ref))
        )
    ]
    for load in proj_loads + loads:
        load.start()
    greet(links, n_exp)

    def token_rows(peer):
        return pl.ds(pl.multiple_of(peer * tokens, tokens), tokens)

    for k, columns in enumerate(column_chunks):
        proj_loads[k].wait()
        part = jnp.dot(gated_ref[...], proj_ref[:, columns], preferred_element_type=jnp.float32)
        partial[:, columns] = part.astype(jnp.bfloat16)
        for gap in range(1, n_exp):
            peer = lax.rem(exp + gap, n_exp)
            links.to_exp(
                partial.at[token_rows(peer), columns],
                sums.at[gap - 1, :, columns],
                sum_sem.at[gap - 1, k],
                peer,
            )
    for k, columns in enumerate(column_chunks):
        mixer_out = partial[token_rows(exp), columns].astype(jnp.float32)
        for gap in range(1, n_exp):
            links.arrived(sums.at[gap - 1, :, columns], sum_sem.at[gap - 1, k])
            mixer_out = mixer_out + sums[gap - 1, :, columns].astype(jnp.float32)
        mixed = residual_ref[:, columns].astype(jnp.float32) + mixer_out
        hidden_one[:, columns] = mixed.astype(jnp.bfloat16)
    hidden_float = hidden_one[...].astype(jnp.float32)
    inv_rms = lax.rsqrt(jnp.mean(hidden_float * hidden_float, axis=-1, keepdims=True) + EPSILON)
    normed = (hidden_float * inv_rms * gain_ref[...]).astype(jnp.bfloat16)
    rows = jnp.dot(select_ref[...], normed, preferred_element_type=jnp.float32)
    dispatch[...] = rows.astype(jnp.bfloat16).reshape(dispatch.shape)

    def rows_of(gap):
        return slots.at[0, pl.ds(gap * cap, cap)]

    for gap in range(1, n_exp):
        peer = lax.rem(exp + gap, n_exp)
        links.to_exp(dispatch.at[peer], rows_of(gap), dispatch_sem.at[gap - 1], peer)
    slots[0, 0:cap] = dispatch[exp]
    gather = Gather(links, slots, gather_sem)
    for half in range(2):
        for gap in range(half * n_exp // 2, (half + 1) * n_exp // 2):
            if gap:
                links.arrived(rows_of(gap), dispatch_sem.at[gap - 1])
        gather.begin(half)
    gather.forward_near()

    tile = 256
    group = 4

    count = group * slots.shape[1]

    def into_hidden(first):
        at = pl.ds(first * slots.shape[1], count)

        @pl.loop(0, gate_ref.shape[1] // tile)
        def _(j):
            columns = pl.ds(pl.multiple_of(j * tile, tile), tile)
            x = slots[first : first + group].reshape(count, slots.shape[2])
            gate = jnp.dot(x, gate_ref[:, columns], preferred_element_type=jnp.float32)
            up = jnp.dot(x, up_ref[:, columns], preferred_element_type=jnp.float32)
            hidden[at, columns] = (jax.nn.silu(gate) * up).astype(jnp.bfloat16)

    def out_of_hidden(first):
        at = pl.ds(first * slots.shape[1], count)

        @pl.loop(0, down_ref.shape[1] // tile)
        def _(j):
            columns = pl.ds(pl.multiple_of(j * tile, tile), tile)
            y = jnp.dot(hidden[at, :], down_ref[:, columns], preferred_element_type=jnp.float32)
            products[first : first + group, :, columns] = y.astype(jnp.bfloat16).reshape(
                group, slots.shape[1], tile
            )

    def pair(mask):
        at = (mask ^ CORE) // 2
        links.to_ctx(products.at[mask], paired.at[at], pair_sem.at[at], CORE)

    for mask in (1, 3):
        gather.wait(mask, 0)
        gather.wait(mask, 1)
    for load in loads:
        load.wait()
    into_hidden(0)
    gather.forward_far()
    for mask in (5, 7):
        gather.wait(mask, 0)
        gather.wait(mask, 1)
    into_hidden(4)
    out_of_hidden(4)
    pair(7)
    pair(5)
    out_of_hidden(0)
    pair(3)
    pair(1)

    def both(mask, rows):
        return products[mask, rows].astype(jnp.float32) + paired[mask // 2, rows].astype(
            jnp.float32
        )

    def store(mask, rows, value):
        products[mask, rows] = value.astype(jnp.bfloat16)

    far = X | Y
    links.arrived(paired.at[far // 2], pair_sem.at[far // 2])
    for half, step in ((0, Y), (1, X)):
        store(far, halves[half], both(far, halves[half]))
        links.to_ctx(products.at[far, halves[half]], relay.at[half], relay_sem.at[half], step)

    def onward(at, step, half):
        links.to_ctx(
            products.at[step, halves[half]],
            last.at[at, halves[half]],
            last_sem.at[at, half],
            step,
        )

    for at, step in ((0, X), (1, Y)):
        half = 1 - at
        links.arrived(paired.at[step // 2], pair_sem.at[step // 2])
        store(step, halves[half], both(step, halves[half]))
        onward(at, step, half)
    for at, step in ((0, X), (1, Y)):
        half = at
        links.arrived(relay.at[half], relay_sem.at[half])
        store(step, halves[half], both(step, halves[half]) + relay[half].astype(jnp.float32))
        onward(at, step, half)
    links.arrived(paired.at[0], pair_sem.at[0])
    for half in range(2):
        value = both(0, halves[half])
        for at in range(2):
            links.arrived(last.at[at, halves[half]], last_sem.at[at, half])
            value = value + last[at, halves[half]].astype(jnp.float32)
        total[halves[half]] = value.astype(jnp.bfloat16)
        for gap in range(half * n_exp // 2, (half + 1) * n_exp // 2):
            mine = total.at[pl.ds(gap * cap, cap)]
            if gap:
                links.to_exp(
                    mine,
                    returned.at[exp],
                    return_sem.at[gap - 1],
                    lax.rem(exp + n_exp - gap, n_exp),
                )
            else:
                returned[exp] = mine[...]
    for gap in range(1, n_exp):
        links.arrived(returned.at[lax.rem(exp + gap, n_exp)], return_sem.at[gap - 1])
    picked = returned[...].reshape(n_exp * cap, returned.shape[2]).astype(jnp.float32)
    moe_out = jnp.dot(
        combine_ref[...],
        picked,
        precision=lax.Precision.HIGHEST,
        preferred_element_type=jnp.float32,
    )
    out_ref[...] = (hidden_one[...].astype(jnp.float32) + moe_out).astype(jnp.bfloat16)
    links.finish()


def fast_experts(
    gated,
    residual,
    norm_gain,
    select,
    combine,
    out_proj,
    gate_proj,
    up_proj,
    down_proj,
    n_exp,
    cap,
):
    tokens, width = residual.shape
    rows = n_exp * cap
    bf16 = jnp.bfloat16
    dma = pltpu.SemaphoreType.DMA
    vmem = pl.BlockSpec(memory_space=pltpu.VMEM)
    sends = (2 + CHUNKS) * (n_exp - 1) + GATHER_SENDS + 4 + 2 + 4
    return pl.pallas_call(
        functools.partial(expert_kernel, n_exp),
        out_shape=jax.ShapeDtypeStruct((tokens, width), bf16),
        in_specs=[vmem] * 5 + [pl.BlockSpec(memory_space=pl.ANY)] * 4,
        out_specs=vmem,
        scratch_shapes=[
            pltpu.VMEM(out_proj.shape, bf16),
            pltpu.VMEM((gated.shape[0], width), bf16),
            pltpu.VMEM((tokens, width), bf16),
            pltpu.VMEM(gate_proj.shape[1:], bf16),
            pltpu.VMEM(up_proj.shape[1:], bf16),
            pltpu.VMEM(down_proj.shape[1:], bf16),
            pltpu.VMEM((n_exp - 1, tokens, width), bf16),
            pltpu.VMEM((n_exp, cap, width), bf16),
            pltpu.VMEM((8, rows, width), bf16),
            pltpu.VMEM((8 * rows, gate_proj.shape[2]), bf16),
            pltpu.VMEM((8, rows, width), bf16),
            pltpu.VMEM((4, rows, width), bf16),
            pltpu.VMEM((2, rows // 2, width), bf16),
            pltpu.VMEM((2, rows, width), bf16),
            pltpu.VMEM((rows, width), bf16),
            pltpu.VMEM((n_exp, cap, width), bf16),
            dma((CHUNKS,)),
            dma((3,)),
            dma((sends,)),
            dma((n_exp - 1, CHUNKS)),
            dma((n_exp - 1,)),
            dma((8, 2)),
            dma((4,)),
            dma((2,)),
            dma((2, 2)),
            dma((n_exp - 1,)),
        ],
        compiler_params=pltpu.CompilerParams(
            collective_id=2, has_side_effects=True, vmem_limit_bytes=48 * 1024 * 1024
        ),
        cost_estimate=pl.CostEstimate(
            flops=6 * 8 * rows * width * gate_proj.shape[2],
            bytes_accessed=6 * width * gate_proj.shape[2],
            transcendentals=0,
        ),
    )(
        gated,
        residual,
        norm_gain.reshape(1, width),
        select,
        combine,
        out_proj,
        gate_proj,
        up_proj,
        down_proj,
    )


def prefix(array, axis, combine, identity):
    count, here = (lax.axis_size(axis), lax.axis_index(axis))
    everything = jax.tree.map(
        lambda part, kind: lax.all_gather(part.astype(kind), axis),
        array,
        (jnp.bfloat16, jnp.bfloat16),
    )
    start = jax.tree.map(
        lambda part, zero: jnp.broadcast_to(jnp.asarray(zero, part.dtype), part.shape),
        array,
        identity,
    )

    def lap(k, before):
        reached = k < here
        new = combine(
            before, jax.tree.map(lambda part, own: part[k].astype(own.dtype), everything, array)
        )
        return jax.tree.map(lambda a, b: jnp.where(reached, a, b), new, before)

    return lax.fori_loop(0, count, lap, start)


def link_states(earlier, later):
    return (earlier[0] * later[0], later[0] * earlier[1] + later[1])


def local_recurrence(step_size, x_float, input_b, output_c, decay_rate):
    tokens = step_size.shape[0]
    width = step_size.shape[1]
    states = decay_rate.shape[0]
    sub_len = tokens // 16
    step_blocks = step_size.reshape(16, sub_len, width)
    x_blocks = x_float.reshape(16, sub_len, width)
    b_blocks = input_b.T.reshape(16, sub_len, states)
    c_blocks = output_c.T.reshape(16, sub_len, states)

    def advance(carry, blocks):
        state, run_step = carry
        step_blk, x_blk, b_blk, c_blk = blocks
        outputs = []
        totals = []
        for inner_pos in range(sub_len):
            step_now = step_blk[inner_pos]
            state = (
                jnp.exp(step_now[None, :] * decay_rate) * state
                + (step_now * x_blk[inner_pos])[None, :] * b_blk[inner_pos][:, None]
            )
            run_step = run_step + step_now
            outputs.append(jnp.sum(c_blk[inner_pos][:, None] * state, axis=0))
            totals.append(run_step)
        return ((state, run_step), (jnp.stack(outputs), jnp.stack(totals)))

    start = (jnp.zeros((states, width), jnp.float32), jnp.zeros((width,), jnp.float32))
    finals, outs = lax.scan(advance, start, (step_blocks, x_blocks, b_blocks, c_blocks))
    local_y = outs[0].reshape(tokens, width)
    cumulative = outs[1].reshape(tokens, width)
    return (finals[0], finals[1], local_y, cumulative)


def on_device(
    mixer_x,
    mixer_z,
    step_raw,
    input_b,
    output_c,
    decay_log,
    skip_gain,
    out_proj,
    residual,
    norm_gain,
    gate_proj,
    up_proj,
    down_proj,
    expert_ids,
    slot_ids,
    route_weight,
):
    n_exp = lax.axis_size("exp")
    step_size = jax.nn.softplus(step_raw)
    decay_rate = -jnp.exp(decay_log)
    x_float = mixer_x.astype(jnp.float32)
    final_state, total_step, local_y, cumulative = local_recurrence(
        step_size, x_float, input_b, output_c, decay_rate
    )
    through_final = jnp.exp(total_step[None, :] * decay_rate)
    identity = (jnp.ones_like(through_final), jnp.zeros_like(final_state))
    tok_dev = residual.shape[0]
    model_width = residual.shape[1]
    experts_local = gate_proj.shape[0]
    experts_all = experts_local * n_exp
    capacity = max(2, expert_ids.shape[1] * tok_dev // experts_all)
    cube = (
        lax.axis_size("ctx") == 8
        and n_exp == 4
        and experts_local == 1
        and capacity % 16 == 0
        and tok_dev % 16 == 0
    )
    if cube:
        carried_state = fast_prefix(through_final, final_state)
    else:
        carried_state = prefix((through_final, final_state), "ctx", link_states, identity)[1]
    correction = jnp.zeros_like(local_y)
    for state_index in range(decay_rate.shape[0]):
        weight_row = (
            jnp.exp(cumulative * decay_rate[state_index][None, :])
            * carried_state[state_index][None, :]
        )
        correction = correction + output_c[state_index][:, None] * weight_row
    mixer_y = local_y + correction + skip_gain * x_float
    gated = (mixer_y * jax.nn.silu(mixer_z.astype(jnp.float32))).astype(jnp.bfloat16)
    slot_count = experts_all * capacity
    per_device = experts_local * capacity
    target_index = jnp.where(slot_ids >= 0, expert_ids * capacity + slot_ids, -1)
    slot_iota = jnp.arange(slot_count, dtype=jnp.int32)
    select = jnp.any(target_index[None, :, :] == slot_iota[:, None, None], axis=-1).astype(
        jnp.bfloat16
    )
    matches = target_index[:, :, None] == slot_iota[None, None, :]
    combine = jnp.sum(
        jnp.where(matches, route_weight[:, :, None], jnp.zeros_like(route_weight)[:, :, None]),
        axis=1,
    )
    if cube:
        return fast_experts(
            gated,
            residual,
            norm_gain,
            select,
            combine,
            out_proj,
            gate_proj,
            up_proj,
            down_proj,
            n_exp,
            capacity,
        )
    partial_out = jnp.dot(gated, out_proj, preferred_element_type=jnp.float32)
    summed = lax.psum(partial_out.astype(jnp.bfloat16), "exp").astype(jnp.float32)
    mixer_out = lax.dynamic_slice_in_dim(summed, lax.axis_index("exp") * tok_dev, tok_dev, 0)
    hidden_one = (residual.astype(jnp.float32) + mixer_out).astype(jnp.bfloat16)
    hidden_one = lax.optimization_barrier(hidden_one)
    hidden_float = hidden_one.astype(jnp.float32)
    inv_rms = lax.rsqrt(jnp.mean(hidden_float * hidden_float, axis=-1, keepdims=True) + EPSILON)
    normed = (hidden_float * inv_rms * norm_gain).astype(jnp.bfloat16)
    dispatch = jnp.dot(select, normed, preferred_element_type=jnp.float32).astype(jnp.bfloat16)
    arrived = lax.all_to_all(
        dispatch.reshape(n_exp, per_device, model_width),
        "exp",
        split_axis=0,
        concat_axis=0,
        tiled=True,
    )
    piece = lax.all_gather(arrived, "ctx", axis=0, tiled=True)
    outputs = []
    local_index = 0
    rows_here = piece.reshape(-1, piece.shape[2])
    gate_value = jnp.dot(rows_here, gate_proj[local_index], preferred_element_type=jnp.float32)
    up_value = jnp.dot(rows_here, up_proj[local_index], preferred_element_type=jnp.float32)
    hidden = (jax.nn.silu(gate_value) * up_value).astype(jnp.bfloat16)
    outputs.append(hidden.reshape(piece.shape[0], capacity, hidden.shape[1]))
    hidden_rows = outputs[0]
    outputs = []
    local_index = 0
    rows_here = hidden_rows.reshape(-1, hidden_rows.shape[2])
    product = jnp.dot(rows_here, down_proj[local_index], preferred_element_type=jnp.float32)
    outputs.append(product.reshape(n_exp * lax.axis_size("ctx"), capacity, model_width))
    expert_out = lax.psum_scatter(
        outputs[0].astype(jnp.bfloat16), "ctx", scatter_dimension=0, tiled=True
    )
    returned = lax.all_to_all(expert_out, "exp", split_axis=0, concat_axis=0, tiled=True).reshape(
        slot_count, model_width
    )
    moe_out = jnp.dot(combine, returned.astype(jnp.float32), precision=lax.Precision.HIGHEST)
    return (hidden_float + moe_out).astype(jnp.bfloat16)


def solution(mesh):
    placed = (
        P("ctx", "exp"),
        P("ctx", "exp"),
        P("ctx", "exp"),
        P(None, "ctx"),
        P(None, "ctx"),
        P(None, "exp"),
        P("exp"),
        P("exp", None),
        P(("ctx", "exp"), None),
        P(),
        P("exp", None, "ctx"),
        P("exp", None, "ctx"),
        P("exp", "ctx", None),
        P(("ctx", "exp"), None),
        P(("ctx", "exp"), None),
        P(("ctx", "exp"), None),
    )
    return jax.shard_map(
        on_device, mesh=mesh, in_specs=placed, out_specs=P(("ctx", "exp"), None), check_vma=False
    )
```

```python
import functools

import jax
import jax.numpy as jnp
from jax import lax
from jax.experimental import pallas as pl
from jax.experimental.pallas import tpu as pltpu
from jax.sharding import PartitionSpec as P

EPSILON = 1e-05


CORE, X, Y = 1, 2, 4
MESH = pl.DeviceIdType.MESH


class Links:
    def __init__(self, send_sem):
        self.ctx = lax.axis_index("ctx")
        self.exp = lax.axis_index("exp")
        self.send_sem = send_sem
        self.sent = []

    def copy(self, src, dst, recv_sem, device):
        made = pltpu.make_async_remote_copy(
            src_ref=src,
            dst_ref=dst,
            send_sem=self.send_sem.at[len(self.sent)],
            recv_sem=recv_sem,
            device_id=device,
            device_id_type=MESH,
        )
        made.start()
        self.sent.append(made)

    def to_ctx(self, src, dst, recv_sem, mask):
        self.copy(src, dst, recv_sem, (self.ctx ^ mask, self.exp))

    def to_exp(self, src, dst, recv_sem, peer):
        self.copy(src, dst, recv_sem, (self.ctx, peer))

    def arrived(self, dst, recv_sem):
        pltpu.make_async_remote_copy(
            src_ref=dst,
            dst_ref=dst,
            send_sem=self.send_sem.at[0],
            recv_sem=recv_sem,
            device_id=(self.ctx ^ CORE, self.exp),
            device_id_type=MESH,
        ).wait_recv()

    def finish(self):
        for made in self.sent:
            made.wait_send()


def greet(links, n_exp):
    barrier = pltpu.get_barrier_semaphore()
    for mask in (CORE, X, Y):
        pl.semaphore_signal(
            barrier, inc=1, device_id=(links.ctx ^ mask, links.exp), device_id_type=MESH
        )
    for gap in range(1, n_exp):
        pl.semaphore_signal(
            barrier,
            inc=1,
            device_id=(links.ctx, lax.rem(links.exp + gap, n_exp)),
            device_id_type=MESH,
        )
    pl.semaphore_wait(barrier, 3 + n_exp - 1)


class Gather:
    def __init__(self, links, slots, sems):
        self.links, self.slots, self.sems = links, slots, sems
        self.half = slots.shape[1] // 2

    def part(self, mask, half):
        return self.slots.at[mask, pl.ds(half * self.half, self.half)]

    def send(self, mask, half, step):
        self.links.to_ctx(
            self.part(mask, half),
            self.part(mask ^ step, half),
            self.sems.at[mask ^ step, half],
            step,
        )

    def wait(self, mask, half):
        self.links.arrived(self.part(mask, half), self.sems.at[mask, half])

    def begin(self, half):
        for step in (X, Y, CORE):
            self.send(0, half, step)

    def forward_near(self):
        self.wait(X, 0)
        self.send(X, 0, Y)
        self.send(X, 0, CORE)
        self.wait(Y, 0)
        self.send(Y, 0, CORE)
        self.wait(Y, 1)
        self.send(Y, 1, X)
        self.send(Y, 1, CORE)
        self.wait(X, 1)
        self.send(X, 1, CORE)

    def forward_far(self):
        for half in range(2):
            self.wait(X | Y, half)
            self.send(X | Y, half, CORE)


GATHER_SENDS = 14
LOG2_E = 1.4426950408889634
CHUNKS = 4


def mixer_kernel(
    raw_ref,
    x_ref,
    b_ref,
    c_ref,
    log_ref,
    y_ref,
    cumulative_ref,
    carried_ref,
    step_ref,
    slots,
    send_sem,
    sems,
):
    links = Links(send_sem)
    greet(links, 1)
    tokens, width = raw_ref.shape
    states, lanes = b_ref.shape[1:]
    decay_two = jnp.exp(log_ref[...]) * (-LOG2_E)

    def over_width(value):
        return jnp.concatenate([value] * (width // lanes), axis=1)

    def advance(j, state):
        rows = pl.ds(pl.multiple_of(j * 8, 8), 8)
        raw = raw_ref[rows, :]
        step = jnp.maximum(raw, 0.0) + jnp.log1p(jnp.exp(-jnp.abs(raw)))
        step_ref[rows, :] = step
        scaled = step * x_ref[rows, :].astype(jnp.float32)
        outputs = []
        for i in range(8):
            here = b_ref[j * 8 + i]
            seen = c_ref[j * 8 + i]
            state = jnp.exp2(step[i : i + 1] * decay_two) * state + scaled[
                i : i + 1
            ] * over_width(here)
            outputs.append(jnp.sum(over_width(seen) * state, axis=0, keepdims=True))
        y_ref[rows, :] = jnp.concatenate(outputs, axis=0)
        return state

    start = jnp.zeros((states, width), jnp.float32)
    final_state = lax.fori_loop(0, tokens // 8, advance, start)
    total_step = jnp.sum(step_ref[...], axis=0, keepdims=True)
    slots[0, 0:states] = jnp.exp2(total_step * decay_two).astype(jnp.bfloat16)
    slots[0, states : 2 * states] = final_state.astype(jnp.bfloat16)
    gather = Gather(links, slots, sems)
    gather.begin(0)
    gather.begin(1)
    row = lax.broadcasted_iota(jnp.int32, (tokens, tokens), 0)
    column = lax.broadcasted_iota(jnp.int32, (tokens, tokens), 1)
    gather.forward_near()
    gather.forward_far()
    cumulative_ref[...] = jnp.dot(
        (column <= row).astype(jnp.float32),
        step_ref[...],
        precision=lax.Precision.HIGHEST,
        preferred_element_type=jnp.float32,
    )
    for mask in (1, 3, 5, 7):
        gather.wait(mask, 0)
        gather.wait(mask, 1)
    state = start
    for k in range(7):
        block = slots[links.ctx ^ k].astype(jnp.float32)
        after = block[:states] * state + block[states:]
        state = jnp.where(k < links.ctx, after, state)
    carried_ref[...] = state
    links.finish()


def fast_mixer(step_raw, mixer_x, input_b, output_c, decay_log):
    tokens, width = step_raw.shape
    states = input_b.shape[0]
    lanes = 128

    def spread(value):
        return jnp.broadcast_to(value.T[:, :, None], (tokens, states, lanes))

    vmem = pl.BlockSpec(memory_space=pltpu.VMEM)
    full = jax.ShapeDtypeStruct((tokens, width), jnp.float32)
    return pl.pallas_call(
        mixer_kernel,
        out_shape=(full, full, jax.ShapeDtypeStruct((states, width), jnp.float32)),
        in_specs=[vmem] * 5,
        out_specs=(vmem, vmem, vmem),
        scratch_shapes=[
            pltpu.VMEM((tokens, width), jnp.float32),
            pltpu.VMEM((8, 2 * states, width), jnp.bfloat16),
            pltpu.SemaphoreType.DMA((GATHER_SENDS,)),
            pltpu.SemaphoreType.DMA((8, 2)),
        ],
        compiler_params=pltpu.CompilerParams(
            collective_id=1, has_side_effects=True, vmem_limit_bytes=24 * 1024 * 1024
        ),
        cost_estimate=pl.CostEstimate(
            flops=8 * tokens * states * width,
            bytes_accessed=16 * tokens * width,
            transcendentals=tokens * states * width,
        ),
    )(step_raw, mixer_x, spread(input_b), spread(output_c), decay_log)


def expert_kernel(
    n_exp,
    gated_ref,
    residual_hbm,
    gain_hbm,
    select_ref,
    combine_ref,
    proj_hbm,
    gate_hbm,
    up_hbm,
    down_hbm,
    out_ref,
    residual_ref,
    gain_ref,
    proj_ref,
    partial,
    hidden_one,
    gate_ref,
    up_ref,
    down_ref,
    sums,
    dispatch,
    slots,
    hidden,
    products,
    paired,
    relay,
    last,
    total,
    returned,
    proj_sem,
    load_sem,
    send_sem,
    sum_sem,
    dispatch_sem,
    gather_sem,
    pair_sem,
    relay_sem,
    last_sem,
    return_sem,
):
    links = Links(send_sem)
    tokens = hidden_one.shape[0]
    cap = dispatch.shape[1]
    half_rows = total.shape[0] // 2
    halves = (pl.ds(0, half_rows), pl.ds(half_rows, half_rows))
    exp = links.exp
    chunk = partial.shape[1] // CHUNKS
    column_chunks = [pl.ds(k * chunk, chunk) for k in range(CHUNKS)]
    proj_loads = [
        pltpu.make_async_copy(proj_hbm.at[:, columns], proj_ref.at[:, columns], proj_sem.at[k])
        for k, columns in enumerate(column_chunks)
    ]
    loads = [
        pltpu.make_async_copy(src.at[0], dst, load_sem.at[k])
        for k, (src, dst) in enumerate(
            ((gate_hbm, gate_ref), (up_hbm, up_ref), (down_hbm, down_ref))
        )
    ]
    row_loads = [
        pltpu.make_async_copy(residual_hbm, residual_ref, load_sem.at[3]),
        pltpu.make_async_copy(gain_hbm, gain_ref, load_sem.at[4]),
    ]
    for load in proj_loads + row_loads + loads:
        load.start()
    greet(links, n_exp)

    def token_rows(peer):
        return pl.ds(pl.multiple_of(peer * tokens, tokens), tokens)

    for k, columns in enumerate(column_chunks):
        proj_loads[k].wait()
        part = jnp.dot(gated_ref[...], proj_ref[:, columns], preferred_element_type=jnp.float32)
        partial[:, columns] = part.astype(jnp.bfloat16)
        for gap in range(1, n_exp):
            peer = lax.rem(exp + gap, n_exp)
            links.to_exp(
                partial.at[token_rows(peer), columns],
                sums.at[gap - 1, :, columns],
                sum_sem.at[gap - 1, k],
                peer,
            )
    for load in row_loads:
        load.wait()
    for k, columns in enumerate(column_chunks):
        mixer_out = partial[token_rows(exp), columns].astype(jnp.float32)
        for gap in range(1, n_exp):
            links.arrived(sums.at[gap - 1, :, columns], sum_sem.at[gap - 1, k])
            mixer_out = mixer_out + sums[gap - 1, :, columns].astype(jnp.float32)
        mixed = residual_ref[:, columns].astype(jnp.float32) + mixer_out
        hidden_one[:, columns] = mixed.astype(jnp.bfloat16)
    hidden_float = hidden_one[...].astype(jnp.float32)
    inv_rms = lax.rsqrt(jnp.mean(hidden_float * hidden_float, axis=-1, keepdims=True) + EPSILON)
    normed = (hidden_float * inv_rms * gain_ref[...]).astype(jnp.bfloat16)
    rows = jnp.dot(select_ref[...], normed, preferred_element_type=jnp.float32)
    dispatch[...] = rows.astype(jnp.bfloat16).reshape(dispatch.shape)

    def rows_of(gap):
        return slots.at[0, pl.ds(gap * cap, cap)]

    for gap in range(1, n_exp):
        peer = lax.rem(exp + gap, n_exp)
        links.to_exp(dispatch.at[peer], rows_of(gap), dispatch_sem.at[gap - 1], peer)
    slots[0, 0:cap] = dispatch[exp]
    gather = Gather(links, slots, gather_sem)
    for half in range(2):
        for gap in range(half * n_exp // 2, (half + 1) * n_exp // 2):
            if gap:
                links.arrived(rows_of(gap), dispatch_sem.at[gap - 1])
        gather.begin(half)
    gather.forward_near()

    tile = 256
    group = 4

    count = group * slots.shape[1]

    def into_hidden(first):
        at = pl.ds(first * slots.shape[1], count)

        @pl.loop(0, gate_ref.shape[1] // tile)
        def _(j):
            columns = pl.ds(pl.multiple_of(j * tile, tile), tile)
            x = slots[first : first + group].reshape(count, slots.shape[2])
            gate = jnp.dot(x, gate_ref[:, columns], preferred_element_type=jnp.float32)
            up = jnp.dot(x, up_ref[:, columns], preferred_element_type=jnp.float32)
            hidden[at, columns] = (jax.nn.silu(gate) * up).astype(jnp.bfloat16)

    def out_of_hidden(first):
        at = pl.ds(first * slots.shape[1], count)

        @pl.loop(0, down_ref.shape[1] // tile)
        def _(j):
            columns = pl.ds(pl.multiple_of(j * tile, tile), tile)
            y = jnp.dot(hidden[at, :], down_ref[:, columns], preferred_element_type=jnp.float32)
            products[first : first + group, :, columns] = y.astype(jnp.bfloat16).reshape(
                group, slots.shape[1], tile
            )

    def pair(mask):
        at = (mask ^ CORE) // 2
        links.to_ctx(products.at[mask], paired.at[at], pair_sem.at[at], CORE)

    for mask in (1, 3):
        gather.wait(mask, 0)
        gather.wait(mask, 1)
    for load in loads:
        load.wait()
    into_hidden(0)
    gather.forward_far()
    for mask in (5, 7):
        gather.wait(mask, 0)
        gather.wait(mask, 1)
    into_hidden(4)
    out_of_hidden(4)
    pair(7)
    pair(5)
    out_of_hidden(0)
    pair(3)
    pair(1)

    def both(mask, rows):
        return products[mask, rows].astype(jnp.float32) + paired[mask // 2, rows].astype(
            jnp.float32
        )

    def store(mask, rows, value):
        products[mask, rows] = value.astype(jnp.bfloat16)

    far = X | Y
    links.arrived(paired.at[far // 2], pair_sem.at[far // 2])
    for half, step in ((0, Y), (1, X)):
        store(far, halves[half], both(far, halves[half]))
        links.to_ctx(products.at[far, halves[half]], relay.at[half], relay_sem.at[half], step)

    def onward(at, step, half):
        links.to_ctx(
            products.at[step, halves[half]],
            last.at[at, halves[half]],
            last_sem.at[at, half],
            step,
        )

    for at, step in ((0, X), (1, Y)):
        half = 1 - at
        links.arrived(paired.at[step // 2], pair_sem.at[step // 2])
        store(step, halves[half], both(step, halves[half]))
        onward(at, step, half)
    for at, step in ((0, X), (1, Y)):
        half = at
        links.arrived(relay.at[half], relay_sem.at[half])
        store(step, halves[half], both(step, halves[half]) + relay[half].astype(jnp.float32))
        onward(at, step, half)
    links.arrived(paired.at[0], pair_sem.at[0])
    for half in range(2):
        value = both(0, halves[half])
        for at in range(2):
            links.arrived(last.at[at, halves[half]], last_sem.at[at, half])
            value = value + last[at, halves[half]].astype(jnp.float32)
        total[halves[half]] = value.astype(jnp.bfloat16)
        for gap in range(half * n_exp // 2, (half + 1) * n_exp // 2):
            mine = total.at[pl.ds(gap * cap, cap)]
            if gap:
                links.to_exp(
                    mine,
                    returned.at[exp],
                    return_sem.at[gap - 1],
                    lax.rem(exp + n_exp - gap, n_exp),
                )
            else:
                returned[exp] = mine[...]
    for gap in range(1, n_exp):
        links.arrived(returned.at[lax.rem(exp + gap, n_exp)], return_sem.at[gap - 1])
    picked = returned[...].reshape(n_exp * cap, returned.shape[2]).astype(jnp.float32)
    moe_out = jnp.dot(
        combine_ref[...],
        picked,
        precision=lax.Precision.HIGHEST,
        preferred_element_type=jnp.float32,
    )
    out_ref[...] = (hidden_one[...].astype(jnp.float32) + moe_out).astype(jnp.bfloat16)
    links.finish()


def fast_experts(
    gated,
    residual,
    norm_gain,
    select,
    combine,
    out_proj,
    gate_proj,
    up_proj,
    down_proj,
    n_exp,
    cap,
):
    tokens, width = residual.shape
    rows = n_exp * cap
    bf16 = jnp.bfloat16
    dma = pltpu.SemaphoreType.DMA
    vmem = pl.BlockSpec(memory_space=pltpu.VMEM)
    hbm = pl.BlockSpec(memory_space=pl.ANY)
    sends = (2 + CHUNKS) * (n_exp - 1) + GATHER_SENDS + 4 + 2 + 4
    return pl.pallas_call(
        functools.partial(expert_kernel, n_exp),
        out_shape=jax.ShapeDtypeStruct((tokens, width), bf16),
        in_specs=[vmem] + [hbm] * 2 + [vmem] * 2 + [hbm] * 4,
        out_specs=vmem,
        scratch_shapes=[
            pltpu.VMEM((tokens, width), bf16),
            pltpu.VMEM((1, width), jnp.float32),
            pltpu.VMEM(out_proj.shape, bf16),
            pltpu.VMEM((gated.shape[0], width), bf16),
            pltpu.VMEM((tokens, width), bf16),
            pltpu.VMEM(gate_proj.shape[1:], bf16),
            pltpu.VMEM(up_proj.shape[1:], bf16),
            pltpu.VMEM(down_proj.shape[1:], bf16),
            pltpu.VMEM((n_exp - 1, tokens, width), bf16),
            pltpu.VMEM((n_exp, cap, width), bf16),
            pltpu.VMEM((8, rows, width), bf16),
            pltpu.VMEM((8 * rows, gate_proj.shape[2]), bf16),
            pltpu.VMEM((8, rows, width), bf16),
            pltpu.VMEM((4, rows, width), bf16),
            pltpu.VMEM((2, rows // 2, width), bf16),
            pltpu.VMEM((2, rows, width), bf16),
            pltpu.VMEM((rows, width), bf16),
            pltpu.VMEM((n_exp, cap, width), bf16),
            dma((CHUNKS,)),
            dma((5,)),
            dma((sends,)),
            dma((n_exp - 1, CHUNKS)),
            dma((n_exp - 1,)),
            dma((8, 2)),
            dma((4,)),
            dma((2,)),
            dma((2, 2)),
            dma((n_exp - 1,)),
        ],
        compiler_params=pltpu.CompilerParams(
            collective_id=2, has_side_effects=True, vmem_limit_bytes=48 * 1024 * 1024
        ),
        cost_estimate=pl.CostEstimate(
            flops=6 * 8 * rows * width * gate_proj.shape[2],
            bytes_accessed=6 * width * gate_proj.shape[2],
            transcendentals=0,
        ),
    )(
        gated,
        residual,
        norm_gain.reshape(1, width),
        select,
        combine,
        out_proj,
        gate_proj,
        up_proj,
        down_proj,
    )


def prefix(array, axis, combine, identity):
    count, here = (lax.axis_size(axis), lax.axis_index(axis))
    everything = jax.tree.map(
        lambda part, kind: lax.all_gather(part.astype(kind), axis),
        array,
        (jnp.bfloat16, jnp.bfloat16),
    )
    start = jax.tree.map(
        lambda part, zero: jnp.broadcast_to(jnp.asarray(zero, part.dtype), part.shape),
        array,
        identity,
    )

    def lap(k, before):
        reached = k < here
        new = combine(
            before, jax.tree.map(lambda part, own: part[k].astype(own.dtype), everything, array)
        )
        return jax.tree.map(lambda a, b: jnp.where(reached, a, b), new, before)

    return lax.fori_loop(0, count, lap, start)


def link_states(earlier, later):
    return (earlier[0] * later[0], later[0] * earlier[1] + later[1])


def local_recurrence(step_size, x_float, input_b, output_c, decay_rate):
    tokens = step_size.shape[0]
    width = step_size.shape[1]
    states = decay_rate.shape[0]
    sub_len = tokens // 16
    step_blocks = step_size.reshape(16, sub_len, width)
    x_blocks = x_float.reshape(16, sub_len, width)
    b_blocks = input_b.T.reshape(16, sub_len, states)
    c_blocks = output_c.T.reshape(16, sub_len, states)

    def advance(carry, blocks):
        state, run_step = carry
        step_blk, x_blk, b_blk, c_blk = blocks
        outputs = []
        totals = []
        for inner_pos in range(sub_len):
            step_now = step_blk[inner_pos]
            state = (
                jnp.exp(step_now[None, :] * decay_rate) * state
                + (step_now * x_blk[inner_pos])[None, :] * b_blk[inner_pos][:, None]
            )
            run_step = run_step + step_now
            outputs.append(jnp.sum(c_blk[inner_pos][:, None] * state, axis=0))
            totals.append(run_step)
        return ((state, run_step), (jnp.stack(outputs), jnp.stack(totals)))

    start = (jnp.zeros((states, width), jnp.float32), jnp.zeros((width,), jnp.float32))
    finals, outs = lax.scan(advance, start, (step_blocks, x_blocks, b_blocks, c_blocks))
    local_y = outs[0].reshape(tokens, width)
    cumulative = outs[1].reshape(tokens, width)
    return (finals[0], finals[1], local_y, cumulative)


def on_device(
    mixer_x,
    mixer_z,
    step_raw,
    input_b,
    output_c,
    decay_log,
    skip_gain,
    out_proj,
    residual,
    norm_gain,
    gate_proj,
    up_proj,
    down_proj,
    expert_ids,
    slot_ids,
    route_weight,
):
    n_exp = lax.axis_size("exp")
    decay_rate = -jnp.exp(decay_log)
    x_float = mixer_x.astype(jnp.float32)
    tok_dev = residual.shape[0]
    model_width = residual.shape[1]
    experts_local = gate_proj.shape[0]
    experts_all = experts_local * n_exp
    capacity = max(2, expert_ids.shape[1] * tok_dev // experts_all)
    cube = (
        lax.axis_size("ctx") == 8
        and n_exp == 4
        and experts_local == 1
        and capacity % 16 == 0
        and tok_dev % 16 == 0
    )
    slot_count = experts_all * capacity
    per_device = experts_local * capacity
    target_index = jnp.where(slot_ids >= 0, expert_ids * capacity + slot_ids, -1)
    slot_iota = jnp.arange(slot_count, dtype=jnp.int32)
    select = jnp.any(target_index[None, :, :] == slot_iota[:, None, None], axis=-1).astype(
        jnp.bfloat16
    )
    matches = target_index[:, :, None] == slot_iota[None, None, :]
    combine = jnp.sum(
        jnp.where(matches, route_weight[:, :, None], jnp.zeros_like(route_weight)[:, :, None]),
        axis=1,
    )
    if cube:
        step_raw, select, combine = lax.optimization_barrier((step_raw, select, combine))
        local_y, cumulative, carried_state = fast_mixer(
            step_raw, mixer_x, input_b, output_c, decay_log
        )
    else:
        step_size = jax.nn.softplus(step_raw)
        final_state, total_step, local_y, cumulative = local_recurrence(
            step_size, x_float, input_b, output_c, decay_rate
        )
        through_final = jnp.exp(total_step[None, :] * decay_rate)
        identity = (jnp.ones_like(through_final), jnp.zeros_like(final_state))
        carried_state = prefix((through_final, final_state), "ctx", link_states, identity)[1]
    correction = jnp.zeros_like(local_y)
    for state_index in range(decay_rate.shape[0]):
        weight_row = (
            jnp.exp(cumulative * decay_rate[state_index][None, :])
            * carried_state[state_index][None, :]
        )
        correction = correction + output_c[state_index][:, None] * weight_row
    mixer_y = local_y + correction + skip_gain * x_float
    gated = (mixer_y * jax.nn.silu(mixer_z.astype(jnp.float32))).astype(jnp.bfloat16)
    if cube:
        return fast_experts(
            gated,
            residual,
            norm_gain,
            select,
            combine,
            out_proj,
            gate_proj,
            up_proj,
            down_proj,
            n_exp,
            capacity,
        )
    partial_out = jnp.dot(gated, out_proj, preferred_element_type=jnp.float32)
    summed = lax.psum(partial_out.astype(jnp.bfloat16), "exp").astype(jnp.float32)
    mixer_out = lax.dynamic_slice_in_dim(summed, lax.axis_index("exp") * tok_dev, tok_dev, 0)
    hidden_one = (residual.astype(jnp.float32) + mixer_out).astype(jnp.bfloat16)
    hidden_one = lax.optimization_barrier(hidden_one)
    hidden_float = hidden_one.astype(jnp.float32)
    inv_rms = lax.rsqrt(jnp.mean(hidden_float * hidden_float, axis=-1, keepdims=True) + EPSILON)
    normed = (hidden_float * inv_rms * norm_gain).astype(jnp.bfloat16)
    dispatch = jnp.dot(select, normed, preferred_element_type=jnp.float32).astype(jnp.bfloat16)
    arrived = lax.all_to_all(
        dispatch.reshape(n_exp, per_device, model_width),
        "exp",
        split_axis=0,
        concat_axis=0,
        tiled=True,
    )
    piece = lax.all_gather(arrived, "ctx", axis=0, tiled=True)
    outputs = []
    local_index = 0
    rows_here = piece.reshape(-1, piece.shape[2])
    gate_value = jnp.dot(rows_here, gate_proj[local_index], preferred_element_type=jnp.float32)
    up_value = jnp.dot(rows_here, up_proj[local_index], preferred_element_type=jnp.float32)
    hidden = (jax.nn.silu(gate_value) * up_value).astype(jnp.bfloat16)
    outputs.append(hidden.reshape(piece.shape[0], capacity, hidden.shape[1]))
    hidden_rows = outputs[0]
    outputs = []
    local_index = 0
    rows_here = hidden_rows.reshape(-1, hidden_rows.shape[2])
    product = jnp.dot(rows_here, down_proj[local_index], preferred_element_type=jnp.float32)
    outputs.append(product.reshape(n_exp * lax.axis_size("ctx"), capacity, model_width))
    expert_out = lax.psum_scatter(
        outputs[0].astype(jnp.bfloat16), "ctx", scatter_dimension=0, tiled=True
    )
    returned = lax.all_to_all(expert_out, "exp", split_axis=0, concat_axis=0, tiled=True).reshape(
        slot_count, model_width
    )
    moe_out = jnp.dot(combine, returned.astype(jnp.float32), precision=lax.Precision.HIGHEST)
    return (hidden_float + moe_out).astype(jnp.bfloat16)


def solution(mesh):
    placed = (
        P("ctx", "exp"),
        P("ctx", "exp"),
        P("ctx", "exp"),
        P(None, "ctx"),
        P(None, "ctx"),
        P(None, "exp"),
        P("exp"),
        P("exp", None),
        P(("ctx", "exp"), None),
        P(),
        P("exp", None, "ctx"),
        P("exp", None, "ctx"),
        P("exp", "ctx", None),
        P(("ctx", "exp"), None),
        P(("ctx", "exp"), None),
        P(("ctx", "exp"), None),
    )
    return jax.shard_map(
        on_device, mesh=mesh, in_specs=placed, out_specs=P(("ctx", "exp"), None), check_vma=False
    )
```

```python
import functools

import jax
import jax.numpy as jnp
from jax import lax
from jax.experimental import pallas as pl
from jax.experimental.pallas import tpu as pltpu
from jax.sharding import PartitionSpec as P

EPSILON = 1e-05


CORE, X, Y = 1, 2, 4
MESH = pl.DeviceIdType.MESH


class Links:
    def __init__(self, send_sem):
        self.ctx = lax.axis_index("ctx")
        self.exp = lax.axis_index("exp")
        self.send_sem = send_sem
        self.sent = []

    def copy(self, src, dst, recv_sem, device):
        made = pltpu.make_async_remote_copy(
            src_ref=src,
            dst_ref=dst,
            send_sem=self.send_sem.at[len(self.sent)],
            recv_sem=recv_sem,
            device_id=device,
            device_id_type=MESH,
        )
        made.start()
        self.sent.append(made)

    def to_ctx(self, src, dst, recv_sem, mask):
        self.copy(src, dst, recv_sem, (self.ctx ^ mask, self.exp))

    def to_exp(self, src, dst, recv_sem, peer):
        self.copy(src, dst, recv_sem, (self.ctx, peer))

    def arrived(self, dst, recv_sem):
        pltpu.make_async_remote_copy(
            src_ref=dst,
            dst_ref=dst,
            send_sem=self.send_sem.at[0],
            recv_sem=recv_sem,
            device_id=(self.ctx ^ CORE, self.exp),
            device_id_type=MESH,
        ).wait_recv()

    def finish(self):
        for made in self.sent:
            made.wait_send()


def greet(links, n_exp):
    barrier = pltpu.get_barrier_semaphore()
    for mask in (CORE, X, Y):
        pl.semaphore_signal(
            barrier, inc=1, device_id=(links.ctx ^ mask, links.exp), device_id_type=MESH
        )
    for gap in range(1, n_exp):
        pl.semaphore_signal(
            barrier,
            inc=1,
            device_id=(links.ctx, lax.rem(links.exp + gap, n_exp)),
            device_id_type=MESH,
        )
    pl.semaphore_wait(barrier, 3 + n_exp - 1)


class Gather:
    def __init__(self, links, slots, sems):
        self.links, self.slots, self.sems = links, slots, sems
        self.half = slots.shape[1] // 2

    def part(self, mask, half):
        return self.slots.at[mask, pl.ds(half * self.half, self.half)]

    def send(self, mask, half, step):
        self.links.to_ctx(
            self.part(mask, half),
            self.part(mask ^ step, half),
            self.sems.at[mask ^ step, half],
            step,
        )

    def wait(self, mask, half):
        self.links.arrived(self.part(mask, half), self.sems.at[mask, half])

    def begin(self, half):
        for step in (X, Y, CORE):
            self.send(0, half, step)

    def forward_near(self):
        self.wait(X, 0)
        self.send(X, 0, Y)
        self.send(X, 0, CORE)
        self.wait(Y, 0)
        self.send(Y, 0, CORE)
        self.wait(Y, 1)
        self.send(Y, 1, X)
        self.send(Y, 1, CORE)
        self.wait(X, 1)
        self.send(X, 1, CORE)

    def forward_far(self):
        for half in range(2):
            self.wait(X | Y, half)
            self.send(X | Y, half, CORE)


GATHER_SENDS = 14
LOG2_E = 1.4426950408889634
CHUNKS = 4


def mixer_kernel(
    raw_ref,
    x_ref,
    b_ref,
    c_ref,
    log_ref,
    y_ref,
    cumulative_ref,
    carried_ref,
    step_ref,
    slots,
    send_sem,
    sems,
):
    links = Links(send_sem)
    greet(links, 1)
    tokens, width = raw_ref.shape
    states, lanes = b_ref.shape[1:]
    decay_two = jnp.exp(log_ref[...]) * (-LOG2_E)

    def over_width(value):
        return jnp.concatenate([value] * (width // lanes), axis=1)

    def advance(j, state):
        rows = pl.ds(pl.multiple_of(j * 8, 8), 8)
        raw = raw_ref[rows, :]
        step = jnp.maximum(raw, 0.0) + jnp.log1p(jnp.exp(-jnp.abs(raw)))
        step_ref[rows, :] = step
        scaled = step * x_ref[rows, :].astype(jnp.float32)
        outputs = []
        for i in range(8):
            here = b_ref[j * 8 + i]
            seen = c_ref[j * 8 + i]
            state = jnp.exp2(step[i : i + 1] * decay_two) * state + scaled[
                i : i + 1
            ] * over_width(here)
            outputs.append(jnp.sum(over_width(seen) * state, axis=0, keepdims=True))
        y_ref[rows, :] = jnp.concatenate(outputs, axis=0)
        return state

    start = jnp.zeros((states, width), jnp.float32)
    final_state = lax.fori_loop(0, tokens // 8, advance, start)
    total_step = jnp.sum(step_ref[...], axis=0, keepdims=True)
    slots[0, 0:states] = jnp.exp2(total_step * decay_two).astype(jnp.bfloat16)
    slots[0, states : 2 * states] = final_state.astype(jnp.bfloat16)
    gather = Gather(links, slots, sems)
    gather.begin(0)
    gather.begin(1)
    row = lax.broadcasted_iota(jnp.int32, (tokens, tokens), 0)
    column = lax.broadcasted_iota(jnp.int32, (tokens, tokens), 1)
    gather.forward_near()
    gather.forward_far()
    cumulative_ref[...] = jnp.dot(
        (column <= row).astype(jnp.float32),
        step_ref[...],
        precision=lax.Precision.HIGHEST,
        preferred_element_type=jnp.float32,
    )
    for mask in (1, 3, 5, 7):
        gather.wait(mask, 0)
        gather.wait(mask, 1)
    state = start
    for k in range(7):
        block = slots[links.ctx ^ k].astype(jnp.float32)
        after = block[:states] * state + block[states:]
        state = jnp.where(k < links.ctx, after, state)
    carried_ref[...] = state
    links.finish()


def fast_mixer(step_raw, mixer_x, input_b, output_c, decay_log):
    tokens, width = step_raw.shape
    states = input_b.shape[0]
    lanes = 128

    def spread(value):
        return jnp.broadcast_to(value.T[:, :, None], (tokens, states, lanes))

    vmem = pl.BlockSpec(memory_space=pltpu.VMEM)
    full = jax.ShapeDtypeStruct((tokens, width), jnp.float32)
    return pl.pallas_call(
        mixer_kernel,
        out_shape=(full, full, jax.ShapeDtypeStruct((states, width), jnp.float32)),
        in_specs=[vmem] * 5,
        out_specs=(vmem, vmem, vmem),
        scratch_shapes=[
            pltpu.VMEM((tokens, width), jnp.float32),
            pltpu.VMEM((8, 2 * states, width), jnp.bfloat16),
            pltpu.SemaphoreType.DMA((GATHER_SENDS,)),
            pltpu.SemaphoreType.DMA((8, 2)),
        ],
        compiler_params=pltpu.CompilerParams(
            collective_id=1, has_side_effects=True, vmem_limit_bytes=24 * 1024 * 1024
        ),
        cost_estimate=pl.CostEstimate(
            flops=8 * tokens * states * width,
            bytes_accessed=16 * tokens * width,
            transcendentals=tokens * states * width,
        ),
    )(step_raw, mixer_x, spread(input_b), spread(output_c), decay_log)


def expert_kernel(
    n_exp,
    gated_ref,
    residual_hbm,
    gain_hbm,
    select_ref,
    combine_ref,
    proj_hbm,
    gate_hbm,
    up_hbm,
    down_hbm,
    out_ref,
    residual_ref,
    gain_ref,
    proj_ref,
    partial,
    hidden_one,
    gate_ref,
    up_ref,
    down_ref,
    sums,
    dispatch,
    slots,
    hidden,
    products,
    paired,
    relay,
    last,
    total,
    returned,
    proj_sem,
    load_sem,
    send_sem,
    sum_sem,
    dispatch_sem,
    gather_sem,
    pair_sem,
    relay_sem,
    last_sem,
    return_sem,
):
    links = Links(send_sem)
    tokens = hidden_one.shape[0]
    cap = dispatch.shape[1]
    half_rows = total.shape[0] // 2
    halves = (pl.ds(0, half_rows), pl.ds(half_rows, half_rows))
    exp = links.exp
    chunk = partial.shape[1] // CHUNKS
    column_chunks = [pl.ds(k * chunk, chunk) for k in range(CHUNKS)]
    proj_loads = [
        pltpu.make_async_copy(proj_hbm.at[:, columns], proj_ref.at[:, columns], proj_sem.at[k])
        for k, columns in enumerate(column_chunks)
    ]
    loads = [
        pltpu.make_async_copy(src.at[0], dst, load_sem.at[k])
        for k, (src, dst) in enumerate(
            ((gate_hbm, gate_ref), (up_hbm, up_ref), (down_hbm, down_ref))
        )
    ]
    row_loads = [
        pltpu.make_async_copy(residual_hbm, residual_ref, load_sem.at[3]),
        pltpu.make_async_copy(gain_hbm, gain_ref, load_sem.at[4]),
    ]
    for load in proj_loads + row_loads + loads:
        load.start()
    greet(links, n_exp)

    def token_rows(peer):
        return pl.ds(pl.multiple_of(peer * tokens, tokens), tokens)

    for k, columns in enumerate(column_chunks):
        proj_loads[k].wait()
        part = jnp.dot(gated_ref[...], proj_ref[:, columns], preferred_element_type=jnp.float32)
        partial[:, columns] = part.astype(jnp.bfloat16)
        for gap in range(1, n_exp):
            peer = lax.rem(exp + gap, n_exp)
            links.to_exp(
                partial.at[token_rows(peer), columns],
                sums.at[gap - 1, :, columns],
                sum_sem.at[gap - 1, k],
                peer,
            )
    for load in row_loads:
        load.wait()
    for k, columns in enumerate(column_chunks):
        mixer_out = partial[token_rows(exp), columns].astype(jnp.float32)
        for gap in range(1, n_exp):
            links.arrived(sums.at[gap - 1, :, columns], sum_sem.at[gap - 1, k])
            mixer_out = mixer_out + sums[gap - 1, :, columns].astype(jnp.float32)
        mixed = residual_ref[:, columns].astype(jnp.float32) + mixer_out
        hidden_one[:, columns] = mixed.astype(jnp.bfloat16)
    hidden_float = hidden_one[...].astype(jnp.float32)
    inv_rms = lax.rsqrt(jnp.mean(hidden_float * hidden_float, axis=-1, keepdims=True) + EPSILON)
    normed = (hidden_float * inv_rms * gain_ref[...]).astype(jnp.bfloat16)
    rows = jnp.dot(select_ref[...], normed, preferred_element_type=jnp.float32)
    dispatch[...] = rows.astype(jnp.bfloat16).reshape(dispatch.shape)

    def rows_of(gap):
        return slots.at[0, pl.ds(gap * cap, cap)]

    for gap in range(1, n_exp):
        peer = lax.rem(exp + gap, n_exp)
        links.to_exp(dispatch.at[peer], rows_of(gap), dispatch_sem.at[gap - 1], peer)
    slots[0, 0:cap] = dispatch[exp]
    gather = Gather(links, slots, gather_sem)
    for half in range(2):
        for gap in range(half * n_exp // 2, (half + 1) * n_exp // 2):
            if gap:
                links.arrived(rows_of(gap), dispatch_sem.at[gap - 1])
        gather.begin(half)
    gather.forward_near()

    tile = 256
    group = 4

    count = group * slots.shape[1]

    def into_hidden(first):
        at = pl.ds(first * slots.shape[1], count)

        @pl.loop(0, gate_ref.shape[1] // tile)
        def _(j):
            columns = pl.ds(pl.multiple_of(j * tile, tile), tile)
            x = slots[first : first + group].reshape(count, slots.shape[2])
            gate = jnp.dot(x, gate_ref[:, columns], preferred_element_type=jnp.float32)
            up = jnp.dot(x, up_ref[:, columns], preferred_element_type=jnp.float32)
            hidden[at, columns] = (jax.nn.silu(gate) * up).astype(jnp.bfloat16)

    def out_of_hidden(first):
        at = pl.ds(first * slots.shape[1], count)

        @pl.loop(0, down_ref.shape[1] // tile)
        def _(j):
            columns = pl.ds(pl.multiple_of(j * tile, tile), tile)
            y = jnp.dot(hidden[at, :], down_ref[:, columns], preferred_element_type=jnp.float32)
            products[first : first + group, :, columns] = y.astype(jnp.bfloat16).reshape(
                group, slots.shape[1], tile
            )

    def pair(mask):
        at = (mask ^ CORE) // 2
        links.to_ctx(products.at[mask], paired.at[at], pair_sem.at[at], CORE)

    for mask in (1, 3):
        gather.wait(mask, 0)
        gather.wait(mask, 1)
    for load in loads:
        load.wait()
    into_hidden(0)
    gather.forward_far()
    for mask in (5, 7):
        gather.wait(mask, 0)
        gather.wait(mask, 1)
    into_hidden(4)
    out_of_hidden(4)
    pair(7)
    pair(5)
    out_of_hidden(0)
    pair(3)
    pair(1)

    def both(mask, rows):
        return products[mask, rows].astype(jnp.float32) + paired[mask // 2, rows].astype(
            jnp.float32
        )

    def store(mask, rows, value):
        products[mask, rows] = value.astype(jnp.bfloat16)

    far = X | Y
    links.arrived(paired.at[far // 2], pair_sem.at[far // 2])
    for half, step in ((0, Y), (1, X)):
        store(far, halves[half], both(far, halves[half]))
        links.to_ctx(products.at[far, halves[half]], relay.at[half], relay_sem.at[half], step)

    def onward(at, step, half):
        links.to_ctx(
            products.at[step, halves[half]],
            last.at[at, halves[half]],
            last_sem.at[at, half],
            step,
        )

    for at, step in ((0, X), (1, Y)):
        half = 1 - at
        links.arrived(paired.at[step // 2], pair_sem.at[step // 2])
        store(step, halves[half], both(step, halves[half]))
        onward(at, step, half)
    for at, step in ((0, X), (1, Y)):
        half = at
        links.arrived(relay.at[half], relay_sem.at[half])
        store(step, halves[half], both(step, halves[half]) + relay[half].astype(jnp.float32))
        onward(at, step, half)
    links.arrived(paired.at[0], pair_sem.at[0])
    for half in range(2):
        value = both(0, halves[half])
        for at in range(2):
            links.arrived(last.at[at, halves[half]], last_sem.at[at, half])
            value = value + last[at, halves[half]].astype(jnp.float32)
        total[halves[half]] = value.astype(jnp.bfloat16)
        for gap in range(half * n_exp // 2, (half + 1) * n_exp // 2):
            mine = total.at[pl.ds(gap * cap, cap)]
            if gap:
                links.to_exp(
                    mine,
                    returned.at[exp],
                    return_sem.at[gap - 1],
                    lax.rem(exp + n_exp - gap, n_exp),
                )
            else:
                returned[exp] = mine[...]
    for gap in range(1, n_exp):
        links.arrived(returned.at[lax.rem(exp + gap, n_exp)], return_sem.at[gap - 1])
    picked = returned[...].reshape(n_exp * cap, returned.shape[2]).astype(jnp.float32)
    moe_out = jnp.dot(
        combine_ref[...],
        picked,
        precision=lax.Precision.HIGHEST,
        preferred_element_type=jnp.float32,
    )
    out_ref[...] = (hidden_one[...].astype(jnp.float32) + moe_out).astype(jnp.bfloat16)
    links.finish()


def fast_experts(
    gated,
    residual,
    norm_gain,
    select,
    combine,
    out_proj,
    gate_proj,
    up_proj,
    down_proj,
    n_exp,
    cap,
):
    tokens, width = residual.shape
    rows = n_exp * cap
    bf16 = jnp.bfloat16
    dma = pltpu.SemaphoreType.DMA
    vmem = pl.BlockSpec(memory_space=pltpu.VMEM)
    hbm = pl.BlockSpec(memory_space=pl.ANY)
    sends = (2 + CHUNKS) * (n_exp - 1) + GATHER_SENDS + 4 + 2 + 4
    return pl.pallas_call(
        functools.partial(expert_kernel, n_exp),
        out_shape=jax.ShapeDtypeStruct((tokens, width), bf16),
        in_specs=[vmem] + [hbm] * 2 + [vmem] * 2 + [hbm] * 4,
        out_specs=vmem,
        scratch_shapes=[
            pltpu.VMEM((tokens, width), bf16),
            pltpu.VMEM((1, width), jnp.float32),
            pltpu.VMEM(out_proj.shape, bf16),
            pltpu.VMEM((gated.shape[0], width), bf16),
            pltpu.VMEM((tokens, width), bf16),
            pltpu.VMEM(gate_proj.shape[1:], bf16),
            pltpu.VMEM(up_proj.shape[1:], bf16),
            pltpu.VMEM(down_proj.shape[1:], bf16),
            pltpu.VMEM((n_exp - 1, tokens, width), bf16),
            pltpu.VMEM((n_exp, cap, width), bf16),
            pltpu.VMEM((8, rows, width), bf16),
            pltpu.VMEM((8 * rows, gate_proj.shape[2]), bf16),
            pltpu.VMEM((8, rows, width), bf16),
            pltpu.VMEM((4, rows, width), bf16),
            pltpu.VMEM((2, rows // 2, width), bf16),
            pltpu.VMEM((2, rows, width), bf16),
            pltpu.VMEM((rows, width), bf16),
            pltpu.VMEM((n_exp, cap, width), bf16),
            dma((CHUNKS,)),
            dma((5,)),
            dma((sends,)),
            dma((n_exp - 1, CHUNKS)),
            dma((n_exp - 1,)),
            dma((8, 2)),
            dma((4,)),
            dma((2,)),
            dma((2, 2)),
            dma((n_exp - 1,)),
        ],
        compiler_params=pltpu.CompilerParams(
            collective_id=2, has_side_effects=True, vmem_limit_bytes=48 * 1024 * 1024
        ),
        cost_estimate=pl.CostEstimate(
            flops=6 * 8 * rows * width * gate_proj.shape[2],
            bytes_accessed=6 * width * gate_proj.shape[2],
            transcendentals=0,
        ),
    )(
        gated,
        residual,
        norm_gain.reshape(1, width),
        select,
        combine,
        out_proj,
        gate_proj,
        up_proj,
        down_proj,
    )


def prefix(array, axis, combine, identity):
    count, here = (lax.axis_size(axis), lax.axis_index(axis))
    everything = jax.tree.map(
        lambda part, kind: lax.all_gather(part.astype(kind), axis),
        array,
        (jnp.bfloat16, jnp.bfloat16),
    )
    start = jax.tree.map(
        lambda part, zero: jnp.broadcast_to(jnp.asarray(zero, part.dtype), part.shape),
        array,
        identity,
    )

    def lap(k, before):
        reached = k < here
        new = combine(
            before, jax.tree.map(lambda part, own: part[k].astype(own.dtype), everything, array)
        )
        return jax.tree.map(lambda a, b: jnp.where(reached, a, b), new, before)

    return lax.fori_loop(0, count, lap, start)


def link_states(earlier, later):
    return (earlier[0] * later[0], later[0] * earlier[1] + later[1])


def local_recurrence(step_size, x_float, input_b, output_c, decay_rate):
    tokens = step_size.shape[0]
    width = step_size.shape[1]
    states = decay_rate.shape[0]
    sub_len = tokens // 16
    step_blocks = step_size.reshape(16, sub_len, width)
    x_blocks = x_float.reshape(16, sub_len, width)
    b_blocks = input_b.T.reshape(16, sub_len, states)
    c_blocks = output_c.T.reshape(16, sub_len, states)

    def advance(carry, blocks):
        state, run_step = carry
        step_blk, x_blk, b_blk, c_blk = blocks
        outputs = []
        totals = []
        for inner_pos in range(sub_len):
            step_now = step_blk[inner_pos]
            state = (
                jnp.exp(step_now[None, :] * decay_rate) * state
                + (step_now * x_blk[inner_pos])[None, :] * b_blk[inner_pos][:, None]
            )
            run_step = run_step + step_now
            outputs.append(jnp.sum(c_blk[inner_pos][:, None] * state, axis=0))
            totals.append(run_step)
        return ((state, run_step), (jnp.stack(outputs), jnp.stack(totals)))

    start = (jnp.zeros((states, width), jnp.float32), jnp.zeros((width,), jnp.float32))
    finals, outs = lax.scan(advance, start, (step_blocks, x_blocks, b_blocks, c_blocks))
    local_y = outs[0].reshape(tokens, width)
    cumulative = outs[1].reshape(tokens, width)
    return (finals[0], finals[1], local_y, cumulative)


def on_device(
    mixer_x,
    mixer_z,
    step_raw,
    input_b,
    output_c,
    decay_log,
    skip_gain,
    out_proj,
    residual,
    norm_gain,
    gate_proj,
    up_proj,
    down_proj,
    expert_ids,
    slot_ids,
    route_weight,
):
    n_exp = lax.axis_size("exp")
    decay_rate = -jnp.exp(decay_log)
    x_float = mixer_x.astype(jnp.float32)
    tok_dev = residual.shape[0]
    model_width = residual.shape[1]
    experts_local = gate_proj.shape[0]
    experts_all = experts_local * n_exp
    capacity = max(2, expert_ids.shape[1] * tok_dev // experts_all)
    cube = (
        lax.axis_size("ctx") == 8
        and n_exp == 4
        and experts_local == 1
        and capacity % 16 == 0
        and tok_dev % 16 == 0
    )
    slot_count = experts_all * capacity
    per_device = experts_local * capacity
    target_index = jnp.where(slot_ids >= 0, expert_ids * capacity + slot_ids, -1)
    slot_iota = jnp.arange(slot_count, dtype=jnp.int32)
    select = jnp.any(target_index[None, :, :] == slot_iota[:, None, None], axis=-1).astype(
        jnp.bfloat16
    )
    matches = target_index[:, :, None] == slot_iota[None, None, :]
    combine = jnp.sum(
        jnp.where(matches, route_weight[:, :, None], jnp.zeros_like(route_weight)[:, :, None]),
        axis=1,
    )
    if cube:
        decay_log, select, combine = lax.optimization_barrier((decay_log, select, combine))
        local_y, cumulative, carried_state = fast_mixer(
            step_raw, mixer_x, input_b, output_c, decay_log
        )
    else:
        step_size = jax.nn.softplus(step_raw)
        final_state, total_step, local_y, cumulative = local_recurrence(
            step_size, x_float, input_b, output_c, decay_rate
        )
        through_final = jnp.exp(total_step[None, :] * decay_rate)
        identity = (jnp.ones_like(through_final), jnp.zeros_like(final_state))
        carried_state = prefix((through_final, final_state), "ctx", link_states, identity)[1]
    correction = jnp.zeros_like(local_y)
    for state_index in range(decay_rate.shape[0]):
        weight_row = (
            jnp.exp(cumulative * decay_rate[state_index][None, :])
            * carried_state[state_index][None, :]
        )
        correction = correction + output_c[state_index][:, None] * weight_row
    mixer_y = local_y + correction + skip_gain * x_float
    gated = (mixer_y * jax.nn.silu(mixer_z.astype(jnp.float32))).astype(jnp.bfloat16)
    if cube:
        return fast_experts(
            gated,
            residual,
            norm_gain,
            select,
            combine,
            out_proj,
            gate_proj,
            up_proj,
            down_proj,
            n_exp,
            capacity,
        )
    partial_out = jnp.dot(gated, out_proj, preferred_element_type=jnp.float32)
    summed = lax.psum(partial_out.astype(jnp.bfloat16), "exp").astype(jnp.float32)
    mixer_out = lax.dynamic_slice_in_dim(summed, lax.axis_index("exp") * tok_dev, tok_dev, 0)
    hidden_one = (residual.astype(jnp.float32) + mixer_out).astype(jnp.bfloat16)
    hidden_one = lax.optimization_barrier(hidden_one)
    hidden_float = hidden_one.astype(jnp.float32)
    inv_rms = lax.rsqrt(jnp.mean(hidden_float * hidden_float, axis=-1, keepdims=True) + EPSILON)
    normed = (hidden_float * inv_rms * norm_gain).astype(jnp.bfloat16)
    dispatch = jnp.dot(select, normed, preferred_element_type=jnp.float32).astype(jnp.bfloat16)
    arrived = lax.all_to_all(
        dispatch.reshape(n_exp, per_device, model_width),
        "exp",
        split_axis=0,
        concat_axis=0,
        tiled=True,
    )
    piece = lax.all_gather(arrived, "ctx", axis=0, tiled=True)
    outputs = []
    local_index = 0
    rows_here = piece.reshape(-1, piece.shape[2])
    gate_value = jnp.dot(rows_here, gate_proj[local_index], preferred_element_type=jnp.float32)
    up_value = jnp.dot(rows_here, up_proj[local_index], preferred_element_type=jnp.float32)
    hidden = (jax.nn.silu(gate_value) * up_value).astype(jnp.bfloat16)
    outputs.append(hidden.reshape(piece.shape[0], capacity, hidden.shape[1]))
    hidden_rows = outputs[0]
    outputs = []
    local_index = 0
    rows_here = hidden_rows.reshape(-1, hidden_rows.shape[2])
    product = jnp.dot(rows_here, down_proj[local_index], preferred_element_type=jnp.float32)
    outputs.append(product.reshape(n_exp * lax.axis_size("ctx"), capacity, model_width))
    expert_out = lax.psum_scatter(
        outputs[0].astype(jnp.bfloat16), "ctx", scatter_dimension=0, tiled=True
    )
    returned = lax.all_to_all(expert_out, "exp", split_axis=0, concat_axis=0, tiled=True).reshape(
        slot_count, model_width
    )
    moe_out = jnp.dot(combine, returned.astype(jnp.float32), precision=lax.Precision.HIGHEST)
    return (hidden_float + moe_out).astype(jnp.bfloat16)


def solution(mesh):
    placed = (
        P("ctx", "exp"),
        P("ctx", "exp"),
        P("ctx", "exp"),
        P(None, "ctx"),
        P(None, "ctx"),
        P(None, "exp"),
        P("exp"),
        P("exp", None),
        P(("ctx", "exp"), None),
        P(),
        P("exp", None, "ctx"),
        P("exp", None, "ctx"),
        P("exp", "ctx", None),
        P(("ctx", "exp"), None),
        P(("ctx", "exp"), None),
        P(("ctx", "exp"), None),
    )
    return jax.shard_map(
        on_device, mesh=mesh, in_specs=placed, out_specs=P(("ctx", "exp"), None), check_vma=False
    )
```
